128 devices in a mesh: gx: 32 (over y, z, core), gy: 4 (over x).
Axes of the slice: x: 4, y: 4, z: 4, core: 2. Of those that a mesh axis runs over, the one named last changes fastest.
Arguments:
- features: bfloat16 [256, 8, 8, 8, 256], P(('gx', 'gy')), may hold values from -6 to 6
- cotangent: bfloat16 [256, 8, 8, 8, 256], P(('gx', 'gy')), may hold values from -6 to 6
- kernel: bfloat16 [27, 256, 256], replicated, may hold values from -0.078125 to 0.078125
- occupancy: int32 [256, 512], P(('gx', 'gy')), may hold values 0 or 1
- neighbors: int32 [256, 27], P(('gx', 'gy')), may hold values from -1 to 1, as said below
Outputs:
- out_features: bfloat16 [256, 8, 8, 8, 256], P(('gx', 'gy'))
- in_grad: bfloat16 [256, 8, 8, 8, 256], P(('gx', 'gy'))
- kernel_grad: float32 [27, 256, 256], replicated
The draws below stay inside these ranges and needn't reach their ends.
Inputs may be any that keep to these rules, and one draw needn't show every extreme that they name: neighbors[b, k] is the slot of the occupied brick at level L + oz in column (cx + ox, cy + oy), where L is brick b's level, and -1 where that column lies outside the 32 x 4 grid or that brick is not occupied; each column holds 2 occupied bricks among 4 levels, slots in rising level; the offset k = 13 entry of a brick is its own slot.
All inputs are finite; a program needn't handle non-finite values. No bound on the sum of `occupancy` on one device may be relied on, other than what follows from the above.
Results may differ from the reference program's by a relative error of at most 0.001.
Values may be sent and summed in bfloat16 or wider, within the bound.
No kernel may reach another device: no remote copies, remote signals or barrier semaphores. Data moves between devices by JAX's collectives and lax.ppermute only.
A program may use at most 128 MiB of HBM per device.

```python
import jax
import jax.numpy as jnp
from jax import lax

C = 256
KOFF = 27
BRICKS_DEV = 2
LEVELS = 4
COLS_X = 32
COLS_Y = 4
BRICKS = 256


def draw_neighbors(key, part):
    key = jax.random.fold_in(key, 7)
    scores = jax.random.randint(key, (COLS_X, COLS_Y, LEVELS), 0, 1 << 20) * LEVELS + jnp.arange(LEVELS, dtype=jnp.int32)
    chosen = jnp.sort(lax.top_k(scores, BRICKS_DEV)[1].astype(jnp.int32), axis=-1)
    hits = (chosen[:, :, :, None] == jnp.arange(LEVELS, dtype=jnp.int32)).astype(jnp.int32)
    slot_of = jnp.where(jnp.sum(hits, axis=2) > 0, jnp.sum(hits * jnp.arange(BRICKS_DEV, dtype=jnp.int32)[:, None], axis=2), -1)
    table = jnp.pad(slot_of, ((1, 1), (1, 1), (1, 1)), constant_values=-1)
    col_x = jnp.arange(COLS_X, dtype=jnp.int32)[:, None, None]
    col_y = jnp.arange(COLS_Y, dtype=jnp.int32)[None, :, None]
    entries = []
    for ox in (-1, 0, 1):
        for oy in (-1, 0, 1):
            for oz in (-1, 0, 1):
                entries.append(table[col_x + 1 + ox, col_y + 1 + oy, chosen + 1 + oz])
    return jnp.stack(entries, -1).reshape(BRICKS, KOFF).astype(jnp.int32)


def touch_ends(array, stream_key, least, top_value):
    longest = array.shape.index(max(array.shape))
    spots = []
    for shift in (0, 1):
        where = [jax.random.randint(jax.random.fold_in(stream_key, axis), (), 0, length) for axis, length in enumerate(array.shape)]
        where[longest] = (where[longest] + shift) % array.shape[longest]
        spots.append(tuple(where))
    return array.at[spots[0]].set(least).at[spots[1]].set(top_value)


def steps_of(stream_key, dims, cuts, least, high):
    def one(dim, shards_of):
        draws = jax.random.uniform(jax.random.fold_in(jax.random.fold_in(stream_key, 6), dim), (shards_of,), jnp.float32, least / len(cuts), high / len(cuts))
        return jnp.repeat(jnp.exp(draws), dims[dim] // shards_of).reshape((-1,) + (1,) * (len(dims) - dim - 1))

    gain = one(*cuts[0])
    for cut in cuts[1:]:
        gain = gain * one(*cut)
    return gain


def gaussian(rng, shape, spread, limit, split=(), kind=jnp.bfloat16):
    loudness = steps_of(rng, shape, split, -0.22, 0.18) if split else 1.0
    values = jax.random.normal(rng, shape, jnp.float32) * spread * loudness
    return jnp.minimum(jnp.maximum(values, -limit), limit).astype(kind)


def setup_inputs(seed: int = 0) -> dict:
    keys = jax.random.split(jax.random.key(seed), 6)
    features = gaussian(keys[0], (BRICKS, 8, 8, 8, C), 1.0, 6.0, ((0, 128),))
    cotangent = gaussian(keys[1], (BRICKS, 8, 8, 8, C), 1.0, 6.0, ((0, 128),))
    kernel = gaussian(keys[2], (KOFF, C, C), (KOFF * C) ** -0.5, 0.078125)
    occupancy = touch_ends((jax.random.randint(keys[3], (BRICKS, 512), 0, 4) < 3).astype(jnp.int32), jax.random.fold_in(keys[3], 1), 0, 1)
    neighbors = draw_neighbors(jax.random.fold_in(keys[5], 71), 0)
    return dict(features=features, cotangent=cotangent, kernel=kernel, occupancy=occupancy, neighbors=neighbors)


layer_pick = {-1: slice(7, 8), 0: slice(0, 8), 1: slice(0, 1)}


def gather_grid(field, neighbors):
    zero = jnp.zeros((1,) + field.shape[1:], field.dtype)
    source = jnp.concatenate([field, zero], 0)
    ids = jnp.arange(BRICKS, dtype=jnp.int32)
    column = ids // BRICKS_DEV
    col_x = column // COLS_Y
    col_y = column % COLS_Y
    x_parts = []
    for ox in (-1, 0, 1):
        y_parts = []
        for oy in (-1, 0, 1):
            z_parts = []
            for oz in (-1, 0, 1):
                offset = 9 * (ox + 1) + 3 * (oy + 1) + (oz + 1)
                slot = neighbors[:, offset].astype(jnp.int32)
                target = ((col_x + ox) * COLS_Y + col_y + oy) * BRICKS_DEV + slot
                target = jnp.where(slot >= 0, target, BRICKS).astype(jnp.int32)
                piece = source[:, layer_pick[ox], layer_pick[oy], layer_pick[oz]]
                z_parts.append(jnp.take(piece, target, axis=0))
            y_parts.append(jnp.concatenate(z_parts, 3))
        x_parts.append(jnp.concatenate(y_parts, 2))
    return jnp.concatenate(x_parts, 1)


def reference(features, cotangent, kernel, occupancy, neighbors):
    mask_b = occupancy.reshape(BRICKS, 8, 8, 8, 1).astype(jnp.bfloat16)
    mask_f = occupancy.reshape(BRICKS * 512, 1).astype(jnp.float32)
    masked = features * mask_b
    masked_grad = cotangent * mask_b
    padded_in = gather_grid(masked, neighbors)
    padded_grad = gather_grid(masked_grad, neighbors)
    flat_grad = masked_grad.reshape(-1, C)
    forward = jnp.zeros((BRICKS * 512, C), jnp.float32)
    backward = jnp.zeros((BRICKS * 512, C), jnp.float32)
    grads = []
    for step_x in range(3):
        for step_y in range(3):
            for step_z in range(3):
                offset = 9 * step_x + 3 * step_y + step_z
                window = padded_in[:, step_x:step_x + 8, step_y:step_y + 8, step_z:step_z + 8].reshape(-1, C)
                forward = forward + jnp.dot(window, kernel[offset], preferred_element_type=jnp.float32)
                grads.append(lax.dot_general(window, flat_grad, (((0,), (0,)), ((), ())), preferred_element_type=jnp.float32))
                back_window = padded_grad[:, 2 - step_x:10 - step_x, 2 - step_y:10 - step_y, 2 - step_z:10 - step_z].reshape(-1, C)
                backward = backward + lax.dot_general(back_window, kernel[offset], (((1,), (1,)), ((), ())), preferred_element_type=jnp.float32)
    out_features = (forward * mask_f).astype(jnp.bfloat16).reshape(BRICKS, 8, 8, 8, C)
    in_grad = (backward * mask_f).astype(jnp.bfloat16).reshape(BRICKS, 8, 8, 8, C)
    kernel_grad = jnp.stack(grads) * jnp.float32(1.0 / (512.0 * BRICKS) ** 0.5)
    return out_features, in_grad, kernel_grad
```

```python
import functools

import jax
import jax.numpy as jnp
import numpy as np
from jax import lax
from jax.experimental import pallas as pl
from jax.experimental.pallas import tpu as pltpu
from jax.sharding import PartitionSpec as P

BOTH = ("gx", "gy")
C = 256
HALF = 128
K = 27
ROWS = 432
BLOCK = 48
BLOCKS = ROWS // BLOCK
CODED = ROWS + 16

VMEM = pl.BlockSpec(memory_space=pltpu.VMEM)
SMEM = pl.BlockSpec(memory_space=pltpu.SMEM)
PARAMS = pltpu.CompilerParams(vmem_limit_bytes=50 * 2**20)

FIRST, SECOND = 0, 1
GROUPS = (
    ((("x", FIRST), ("y", FIRST)), (("z", FIRST), ("x", SECOND)), (("y", SECOND), ("z", SECOND))),
    ((("x", SECOND), ("y", SECOND)), (("z", SECOND), ("x", FIRST)), (("y", FIRST), ("z", FIRST))),
)


def paired(v, pairing):
    return v ^ 1 if pairing == FIRST else 3 - v


def pair_bit(v, pairing):
    return (v ^ (v >> 1)) & 1 if pairing == FIRST else v >> 1


def number(at):
    return ((at["y"] * 4 + at["z"]) * 2 + at["core"]) * 4 + at["x"]


def places():
    for y in range(4):
        for z in range(4):
            for core in range(2):
                for x in range(4):
                    yield {"x": x, "y": y, "z": z, "core": core}


def partners(level, member):
    pairs = []
    for at in places():
        to = dict(at)
        for bit, (axis, pairing) in enumerate(GROUPS[at["core"]][level]):
            if member >> bit & 1:
                to[axis] = paired(to[axis], pairing)
        pairs.append((number(at), number(to)))
    return pairs


def other_core():
    return [(number(at), number({**at, "core": 1 - at["core"]})) for at in places()]


def rank_in(level, core, at):
    ranks = []
    for c in range(2):
        (a, pa), (b, pb) = GROUPS[c][level]
        ranks.append(pair_bit(at[a], pa) + 2 * pair_bit(at[b], pb))
    return jnp.where(core == 0, ranks[0], ranks[1])


def exchange(arrays, level):
    return [lax.ppermute(a, BOTH, partners(level, m + 1)) for m, a in enumerate(arrays)]


def call(kernel, outs, ins, *args, flops=0, scratch=()):
    size = sum(a.size * a.dtype.itemsize for a in args) + sum(o.size * o.dtype.itemsize for o in outs)
    return pl.pallas_call(
        kernel,
        out_shape=list(outs),
        in_specs=list(ins),
        out_specs=[VMEM] * len(outs),
        scratch_shapes=list(scratch),
        compiler_params=PARAMS,
        cost_estimate=pl.CostEstimate(flops=flops, bytes_accessed=size, transcendentals=0),
    )(*args)


def shape(dims, dtype):
    return jax.ShapeDtypeStruct(dims, dtype)


def put_coded(read, write):
    row = lax.broadcasted_iota(jnp.int32, (16, HALF), 0)
    exponents = jnp.zeros((16, HALF), jnp.float32)
    for b in range(BLOCKS):
        x = read(b)
        top = jnp.max(jnp.abs(x), axis=0, keepdims=True)
        e = jnp.ceil(jnp.log2(jnp.maximum(top, 2.0**-110)))
        q = jnp.clip(jnp.round(x * jnp.exp2(15.0 - e)), -32767.0, 32767.0)
        write(b * BLOCK, q.astype(jnp.int16))
        exponents = jnp.where(row == b, e, exponents)
    write(ROWS, exponents.astype(jnp.int16))


def scales_of(tile):
    return jnp.exp2(tile.astype(jnp.float32) - 15.0)


def block_of(ref, index, b):
    return ref[index, b * BLOCK : (b + 1) * BLOCK, :]


def coded_block(ref, index, scales, b):
    return block_of(ref, index, b).astype(jnp.float32) * scales[b : b + 1, :]


def coded_scales(ref, index):
    return scales_of(ref[index, ROWS:CODED, :])


def coded_writer(ref, index):
    def write(start, rows):
        ref[index, start : start + rows.shape[0], :] = rows

    return write


def pair_sum_kernel(rank, own, got, keep, first, second, third):
    g = rank[0]
    for m, out in enumerate((keep, first, second, third)):

        def chunk(c, _, m=m, out=out):
            at = (g ^ m) * 4 + c
            scales = coded_scales(got, at)

            def read(b):
                return block_of(own, at, b) + coded_block(got, at, scales, b)

            if m == 0:
                for b in range(BLOCKS):
                    out[c, b * BLOCK : (b + 1) * BLOCK, :] = read(b)
            else:
                put_coded(read, coded_writer(out, c))
            return 0

        lax.fori_loop(0, 4, chunk, 0)


def group_sum_kernel(rank, own, got_1, got_2, got_3, keep, first, second, third):
    g = rank[0]
    for m, out in enumerate((keep, first, second, third)):
        at = g ^ m
        scales = [coded_scales(r, at) for r in (got_1, got_2, got_3)]

        def read(b, at=at, scales=scales):
            x = block_of(own, at, b)
            for r, s in zip((got_1, got_2, got_3), scales):
                x = x + coded_block(r, at, s, b)
            return x

        if m == 0:
            for b in range(BLOCKS):
                out[0, b * BLOCK : (b + 1) * BLOCK, :] = read(b)
        else:
            put_coded(read, coded_writer(out, 0))


def last_group_kernel(own, got_1, got_2, got_3, out):
    scales = [coded_scales(r, 0) for r in (got_1, got_2, got_3)]

    def read(b):
        x = block_of(own, 0, b)
        for r, s in zip((got_1, got_2, got_3), scales):
            x = x + coded_block(r, 0, s, b)
        return x

    put_coded(read, coded_writer(out, 0))


def total_kernel(own, got_1, got_2, got_3, out):
    refs = (own, got_1, got_2, got_3)
    scales = [coded_scales(r, 0) for r in refs]

    def read(b):
        a = [coded_block(r, 0, s, b) for r, s in zip(refs, scales)]
        return (a[0] + a[1]) + (a[2] + a[3])

    put_coded(read, coded_writer(out, 0))


def finish_kernel(scale, where, a0, a1, a2, a3, b0, b1, b2, b3, out):
    core, inner = where[0], where[1]
    for side, refs in enumerate(((a0, a1, a2, a3), (b0, b1, b2, b3))):
        column = pl.multiple_of((core ^ side) * HALF, HALF)
        outer = where[2 + side]
        inner = where[4 + side]
        for m, ref in enumerate(refs):

            def chunk(c, _, ref=ref, m=m, outer=outer, inner=inner, column=column):
                scales = coded_scales(ref, c) * scale
                start = ((outer ^ m) * 4 + (inner ^ c)) * ROWS
                for b in range(BLOCKS):
                    rows = pl.ds(pl.multiple_of(start + b * BLOCK, 16), BLOCK)
                    out[rows, pl.ds(column, HALF)] = coded_block(ref, c, scales, b)
                return 0

            lax.fori_loop(0, 4, chunk, 0)


def widen(pick, cells, y_low, y_high, x_low, x_high, wide):
    for x in range(10):
        if x == 0:
            layer, side = x_low[...].reshape(160, C), 0
        elif x == 9:
            layer, side = x_high[...].reshape(160, C), 2
        else:
            layer = jnp.concatenate([y_low[x - 1], cells[x - 1].reshape(128, C), y_high[x - 1]], axis=0)
            side = 1
        moved = jnp.dot(pick[side], layer, preferred_element_type=jnp.float32).astype(jnp.bfloat16)
        for oz in range(3):
            wide[oz, x] = moved[160 * oz : 160 * (oz + 1)].reshape(10, 16, C)


def window_of(wide, ox, oy, oz, start, count):
    return wide[oz, pl.ds(ox + start, count), pl.ds(oy, 8)].reshape(count * 128, C)


def kernel_grad_kernel(pick, cells, y_low, y_high, x_low, x_high, grad, own, coded, wide, terms):
    widen(pick, cells, y_low, y_high, x_low, x_high, wide)
    g = grad[...].reshape(1024, C)

    def step(k, _):
        w = window_of(wide, k // 9, (k // 3) % 3, k % 3, 0, 8)
        t = lax.dot_general(w, g, (((0,), (0,)), ((), ())), preferred_element_type=jnp.float32)
        terms[pl.ds(pl.multiple_of(k * C, C), C), :] = t
        return 0

    lax.fori_loop(0, K, step, 0)

    def chunk(c, _):
        def read(b, lanes):
            return terms[pl.ds(pl.multiple_of(c * ROWS + b * BLOCK, 16), BLOCK), lanes]

        for b in range(BLOCKS):
            own[c, b * BLOCK : (b + 1) * BLOCK, :] = read(b, slice(0, HALF))
        put_coded(lambda b: read(b, slice(HALF, C)), coded_writer(coded, c))
        return 0

    lax.fori_loop(0, 16, chunk, 0)


def convolve_kernel(back, pick, cells, y_low, y_high, x_low, x_high, mask, kernel, out, wide, total):
    widen(pick, cells, y_low, y_high, x_low, x_high, wide)
    total[...] = jnp.zeros_like(total)

    def step(k, _):
        ox, oy, oz = k // 9, (k // 3) % 3, k % 3
        if back:
            ox, oy, oz = 2 - ox, 2 - oy, 2 - oz
        w = window_of(wide, ox, oy, oz, 0, 8)
        total[...] += lax.dot_general(
            w, kernel[k], (((1,), (1 if back else 0,)), ((), ())), preferred_element_type=jnp.float32
        )
        return 0

    lax.fori_loop(0, K, step, 0)
    out[...] = (total[...] * mask[...].reshape(1024, 1)).astype(jnp.bfloat16).reshape(8, 8, 16, C)


def picks(neighbors):
    n = neighbors.reshape(2, 3, 3, 3).transpose(1, 2, 0, 3)
    n = jnp.concatenate([n[:, :1]] + [n[:, 1:2]] * 8 + [n[:, 2:]], axis=1)
    z = np.arange(8)[None, :] + np.arange(3)[:, None] - 1
    beyond = (z > 7).astype(np.int32) - (z < 0).astype(np.int32)
    beyond = jnp.asarray(beyond)[None, :, None, None, :]
    n = n[:, None, :, :, None, :]
    slot = jnp.where(beyond < 0, n[..., 0], jnp.where(beyond > 0, n[..., 2], n[..., 1]))
    inside = jnp.asarray(z % 8)[None, :, None, None, :]
    target = slot * 8 + inside + jnp.arange(10, dtype=jnp.int32)[None, None, :, None, None] * 16
    target = jnp.where(slot >= 0, target, -1).reshape(3, 480, 1)
    return (target == jnp.arange(160, dtype=jnp.int32)).astype(jnp.bfloat16)


def shards(features, cotangent, kernel, occupancy, neighbors):
    gx, gy = lax.axis_index("gx"), lax.axis_index("gy")
    core = gx % 2
    at = {"x": gy, "y": gx // 8, "z": (gx // 2) % 4}
    scale = 1.0 / (512.0 * 256.0) ** 0.5

    def cells_of(a):
        return a.transpose(1, 2, 0, 3, 4).reshape(8, 8, 16, C)

    mask = occupancy.reshape(2, 8, 8, 8).transpose(1, 2, 0, 3).reshape(8, 8, 16, 1)
    mask_b = mask.astype(jnp.bfloat16)
    mask_f = mask.astype(jnp.float32)
    cells = cells_of(features) * mask_b
    grad = cells_of(cotangent) * mask_b
    both = jnp.stack([cells, grad])
    up_x = [(i, i + 1) for i in range(31)]
    down_x = [(i + 1, i) for i in range(31)]
    up_y = [(i, i + 1) for i in range(3)]
    down_y = [(i + 1, i) for i in range(3)]
    y_low = lax.ppermute(both[:, :, 7], "gy", up_y)
    y_high = lax.ppermute(both[:, :, 0], "gy", down_y)

    def layer(x):
        return jnp.concatenate([y_low[:, x, None], both[:, x], y_high[:, x, None]], axis=1)

    x_low = lax.ppermute(layer(7), "gx", up_x)
    x_high = lax.ppermute(layer(0), "gx", down_x)
    pick = picks(neighbors)

    grad_halves = jnp.where(core == 0, grad, jnp.concatenate([grad[..., HALF:], grad[..., :HALF]], axis=-1))
    wide = pltpu.VMEM((3, 10, 10, 16, C), jnp.bfloat16)
    flops = 2 * K * 1024 * C * C
    own, coded = call(
        kernel_grad_kernel,
        [shape((16, ROWS, HALF), jnp.float32), shape((16, CODED, HALF), jnp.int16)],
        [VMEM] * 7,
        pick, cells, y_low[0], y_high[0], x_low[0], x_high[0], grad_halves,
        flops=flops,
        scratch=[wide, pltpu.VMEM((K * C, C), jnp.float32)],
    )

    def convolve(back, a, index):
        return call(
            functools.partial(convolve_kernel, back),
            [shape((8, 8, 16, C), jnp.bfloat16)],
            [VMEM] * 8,
            pick, a, y_low[index], y_high[index], x_low[index], x_high[index], mask_f, kernel,
            flops=flops,
            scratch=[wide, pltpu.VMEM((1024, C), jnp.float32)],
        )[0]

    forward = convolve(False, cells, 0)
    backward = convolve(True, grad, 1)

    got = lax.ppermute(coded, BOTH, other_core())
    outer, inner = rank_in(0, core, at), rank_in(1, core, at)
    coded_4 = shape((4, CODED, HALF), jnp.int16)
    coded_1 = shape((1, CODED, HALF), jnp.int16)
    keep, *sent = call(
        pair_sum_kernel,
        [shape((4, ROWS, HALF), jnp.float32)] + [coded_4] * 3,
        [SMEM, VMEM, VMEM],
        outer.reshape(1), own, got,
    )
    keep, *sent = call(
        group_sum_kernel,
        [shape((1, ROWS, HALF), jnp.float32)] + [coded_1] * 3,
        [SMEM] + [VMEM] * 4,
        inner.reshape(1), keep, *exchange(sent, 0),
    )
    (part,) = call(last_group_kernel, [coded_1], [VMEM] * 4, keep, *exchange(sent, 1))
    (whole,) = call(total_kernel, [coded_1], [VMEM] * 4, part, *exchange([part] * 3, 2))
    four = jnp.concatenate([whole] + exchange([whole] * 3, 1))
    sets = [four] + exchange([four] * 3, 0)
    others = [lax.ppermute(s, BOTH, other_core()) for s in sets]
    where = jnp.stack(
        [core, inner, outer, rank_in(0, 1 - core, at), inner, rank_in(1, 1 - core, at)]
    ).astype(jnp.int32)
    (kernel_grad,) = call(
        functools.partial(finish_kernel, scale),
        [shape((K * C, C), jnp.float32)],
        [SMEM] + [VMEM] * 8,
        where, *sets, *others,
    )

    def bricks_of(a):
        return a.reshape(8, 8, 2, 8, C).transpose(2, 0, 1, 3, 4)

    return bricks_of(forward), bricks_of(backward), kernel_grad.reshape(K, C, C)


def solution(mesh):
    placed = (
        P(BOTH, None, None, None, None),
        P(BOTH, None, None, None, None),
        P(),
        P(BOTH, None),
        P(BOTH, None),
    )
    return jax.shard_map(
        shards,
        mesh=mesh,
        in_specs=placed,
        out_specs=(P(BOTH, None, None, None, None), P(BOTH, None, None, None, None), P()),
        check_vma=False,
    )
```

```python
import functools

import jax
import jax.numpy as jnp
from jax import lax
from jax.experimental import pallas as pl
from jax.experimental.pallas import tpu as pltpu
from jax.sharding import PartitionSpec as P

BOTH = ("gx", "gy")
C = 256
HALF = 128
K = 27
EACH = 7
ROWS = 224
BLOCK = 32
BLOCKS = ROWS // BLOCK
CODED = ROWS + 16

CODED_4 = jax.ShapeDtypeStruct((4, CODED, C), jnp.int16)
CODED_1 = jax.ShapeDtypeStruct((1, CODED, C), jnp.int16)

VMEM = pl.BlockSpec(memory_space=pltpu.VMEM)
HBM = pl.BlockSpec(memory_space=pltpu.HBM)
SMEM = pl.BlockSpec(memory_space=pltpu.SMEM)
PARAMS = pltpu.CompilerParams(vmem_limit_bytes=28 * 2**20)

FIRST, SECOND = 0, 1
GROUPS = (
    ((("x", FIRST), ("y", FIRST)), (("z", FIRST), ("x", SECOND)), (("y", SECOND), ("z", SECOND))),
    ((("z", FIRST), ("y", SECOND)), (("x", FIRST), ("y", FIRST)), (("x", SECOND), ("z", SECOND))),
)


def paired(v, pairing):
    return v ^ 1 if pairing == FIRST else 3 - v


def pair_bit(v, pairing):
    return (v ^ (v >> 1)) & 1 if pairing == FIRST else v >> 1


def number(at):
    return ((at["y"] * 4 + at["z"]) * 2 + at["core"]) * 4 + at["x"]


def places():
    for y in range(4):
        for z in range(4):
            for core in range(2):
                for x in range(4):
                    yield {"x": x, "y": y, "z": z, "core": core}


def partners(level, member):
    pairs = []
    for at in places():
        to = dict(at)
        for i, (axis, pairing) in enumerate(GROUPS[at["core"]][level]):
            if member in ((1, 2), (1, 3))[i]:
                to[axis] = paired(to[axis], pairing)
        pairs.append((number(at), number(to)))
    return pairs


def other_core():
    return [(number(at), number({**at, "core": 1 - at["core"]})) for at in places()]


def rank_in(level, core, at):
    ranks = []
    for c in range(2):
        (a, pa), (b, pb) = GROUPS[c][level]
        u, v = pair_bit(at[a], pa), pair_bit(at[b], pb)
        ranks.append(2 * (u ^ v) + v)
    return jnp.where(core == 0, ranks[0], ranks[1])


def exchange(arrays, level):
    return [lax.ppermute(a, BOTH, partners(level, m + 1)) for m, a in enumerate(arrays)]


def after(value, *others):
    return lax.optimization_barrier((value, *others))[0]


def call(kernel, outs, *args, flops=0, scratch=(), space=None):
    size = sum(a.size * a.dtype.itemsize for a in args) + sum(o.size * o.dtype.itemsize for o in outs)
    return pl.pallas_call(
        kernel,
        out_shape=list(outs),
        in_specs=[SMEM if a.dtype == jnp.int32 and a.size < 100 else space or VMEM for a in args],
        out_specs=[VMEM] * len(outs),
        scratch_shapes=list(scratch),
        compiler_params=PARAMS,
        cost_estimate=pl.CostEstimate(flops=flops, bytes_accessed=size, transcendentals=0),
    )(*args)


def shape(dims, dtype):
    return jax.ShapeDtypeStruct(dims, dtype)


def put_coded(read, ref, index):
    row = lax.broadcasted_iota(jnp.int32, (16, C), 0)
    exponents = jnp.zeros((16, C), jnp.float32)
    for b in range(BLOCKS):
        x = read(b)
        top = jnp.max(jnp.abs(x), axis=0, keepdims=True)
        e = jnp.ceil(jnp.log2(jnp.maximum(top, 2.0**-110)))
        q = jnp.clip(jnp.round(x * jnp.exp2(15.0 - e)), -32767.0, 32767.0)
        ref[index, b * BLOCK : (b + 1) * BLOCK, :] = q.astype(jnp.int16)
        exponents = jnp.where(row == b, e, exponents)
    ref[index, ROWS:CODED, :] = exponents.astype(jnp.int16)


def coded_scales(ref, index):
    return jnp.exp2(ref[index, ROWS:CODED, :].astype(jnp.float32) - 15.0)


def block_of(ref, index, b):
    return ref[index, b * BLOCK : (b + 1) * BLOCK, :]


def coded_block(ref, index, scales, b):
    return block_of(ref, index, b).astype(jnp.float32) * scales[b : b + 1, :]


def pair_sum_kernel(last, own, got, out):
    for c in range(4):
        scales = coded_scales(got, c)

        def read(b, c=c, scales=scales):
            rows = slice(c * ROWS + b * BLOCK, c * ROWS + (b + 1) * BLOCK)
            return own[rows, :] + coded_block(got, c, scales, b)

        if last:
            for b in range(BLOCKS):
                out[c, b * BLOCK : (b + 1) * BLOCK, :] = read(b)
        else:
            put_coded(read, out, c)


def group_sum_kernel(rank, own, got_1, got_2, got_3, keep, first, second, third):
    g = rank[0]
    for m, out in enumerate((keep, first, second, third)):
        at = g ^ m
        scales = [coded_scales(r, at) for r in (got_1, got_2, got_3)]

        def read(b, at=at, scales=scales):
            x = block_of(own, at, b)
            for r, s in zip((got_1, got_2, got_3), scales):
                x = x + coded_block(r, at, s, b)
            return x

        if m == 0:
            for b in range(BLOCKS):
                out[0, b * BLOCK : (b + 1) * BLOCK, :] = read(b)
        else:
            put_coded(read, out, 0)


def last_group_kernel(own, got_1, got_2, got_3, out):
    scales = [coded_scales(r, 0) for r in (got_1, got_2, got_3)]

    def read(b):
        x = block_of(own, 0, b)
        for r, s in zip((got_1, got_2, got_3), scales):
            x = x + coded_block(r, 0, s, b)
        return x

    put_coded(read, out, 0)


def total_kernel(own, got_1, got_2, got_3, out):
    refs = (own, got_1, got_2, got_3)
    scales = [coded_scales(r, 0) for r in refs]

    def read(b):
        a = [coded_block(r, 0, s, b) for r, s in zip(refs, scales)]
        return (a[0] + a[1]) + (a[2] + a[3])

    put_coded(read, out, 0)


def finish_kernel(scale, parts, where, *refs):
    n = len(parts)
    out, stage, done = refs[-3:]

    def copy_of(s, j):
        side, member = parts[s]
        k = (where[2 + side] ^ member) * EACH + j
        rows = pl.ds(pl.multiple_of((where[0] ^ side) * HALF, HALF), HALF)
        copy = pltpu.make_async_copy(stage.at[s, j], out.at[jnp.minimum(k, K - 1), rows, :], done.at[s, j])
        return k, copy

    def each(s, j, act):
        k, copy = copy_of(s, j)
        if j < EACH - 1:
            act(copy)
        else:
            pl.when(k < K)(lambda: act(copy))

    for s in range(n):
        for place in range(4):
            c = where[4 + parts[s][0]] ^ place
            scales = coded_scales(refs[s], c) * scale
            for b in range(BLOCKS):
                at = place * BLOCKS + b
                stage[s, at // 4, at % 4 * BLOCK : (at % 4 + 1) * BLOCK, :] = coded_block(refs[s], c, scales, b)
                if at % 4 == 3:
                    each(s, at // 4, lambda copy: copy.start())
    for s in range(n):
        for j in range(EACH):
            each(s, j, lambda copy: copy.wait())


def finish(scale, where, parts, sets, before):
    more = [] if before is None else [before]
    n = len(sets)
    return pl.pallas_call(
        functools.partial(finish_kernel, scale, parts),
        out_shape=shape((K, C, C), jnp.float32),
        in_specs=[SMEM] + [VMEM] * n + [HBM] * len(more),
        out_specs=HBM,
        scratch_shapes=[pltpu.VMEM((n, EACH, HALF, C), jnp.float32), pltpu.SemaphoreType.DMA((n, EACH))],
        input_output_aliases={1 + n: 0} if more else {},
        compiler_params=PARAMS,
        cost_estimate=pl.CostEstimate(flops=0, bytes_accessed=n * EACH * HALF * C * 6, transcendentals=0),
    )(where, *sets, *more)


def prepare_kernel(odd, features, cotangent, occupancy, cells, grad, masks, y_a, y_b):
    r = lax.broadcasted_iota(jnp.int32, (128, 128), 0)
    c = lax.broadcasted_iota(jnp.int32, (128, 128), 1)
    same = (r >> 4 == (c >> 3) & 7) & ((r >> 3) & 1 == c >> 6) & (r & 7 == c & 7)
    low = lax.broadcasted_iota(jnp.int32, (1, 128), 1) < 64
    occupied = occupancy[...].astype(jnp.float32)
    turned = pltpu.roll(occupied, 64, 1)
    even = odd[0] == 0
    for x in range(8):
        lanes = slice(128 * (x // 2), 128 * (x // 2) + 128)
        if x % 2 == 0:
            row = jnp.where(low, occupied[0:1, lanes], turned[1:2, lanes])
        else:
            after_it = slice((lanes.start + 128) % 512, (lanes.start + 128) % 512 + 128)
            row = jnp.where(low, turned[0:1, after_it], occupied[1:2, lanes])
        pick = jnp.where(same, row, 0.0).astype(jnp.bfloat16)
        masks[x] = pick
        for index, (source, out) in enumerate(((features, cells), (cotangent, grad))):
            layer = jnp.concatenate([source[0, x], source[1, x]], axis=0)
            made = jnp.dot(pick, layer, preferred_element_type=jnp.float32).astype(jnp.bfloat16)
            made = made.reshape(8, 16, C)
            out[x] = made
            y_a[index, x] = jnp.where(even, made[7], made[0])
            y_b[index, x] = jnp.where(even, made[0], made[7])


def picks_kernel(neighbors, out):
    r = lax.broadcasted_iota(jnp.int32, (160, 160), 0)
    c = lax.broadcasted_iota(jnp.int32, (160, 160), 1)
    y, s, z = r >> 4, (r >> 3) & 1, r & 7
    same = y == c >> 4
    side_y = jnp.where(y == 0, 0, jnp.where(y == 9, 2, 1))
    which = side_y * 2 + s
    for ox in range(3):
        for oz in range(3):
            edge = z == (0 if oz == 0 else 7)
            slot = jnp.full((160, 160), -1, jnp.int32)
            for oy in range(3):
                for brick in range(2):
                    level = neighbors[brick, 9 * ox + 3 * oy + 1]
                    beyond = neighbors[brick, 9 * ox + 3 * oy + oz]
                    found = jnp.where(edge, beyond, level) if oz != 1 else level
                    slot = jnp.where(which == 2 * oy + brick, found, slot)
            hit = same & (slot >= 0) & ((c & 15) == slot * 8 + ((z + oz - 1) & 7))
            out[ox, 160 * oz : 160 * (oz + 1), :] = jnp.where(hit, 1.0, 0.0).astype(jnp.bfloat16)


def edges_kernel(odd, cells, grad, y_a, y_b, x_a, x_b):
    even = odd[0] == 0
    for out, x in ((x_a, jnp.where(odd[1] == 0, 7, 0)), (x_b, jnp.where(odd[1] == 0, 0, 7))):
        for i, a in enumerate((cells, grad)):
            out[i, 0] = jnp.where(even, y_b[i, x], y_a[i, x])
            out[i, 1:9] = a[x]
            out[i, 9] = jnp.where(even, y_a[i, x], y_b[i, x])


def widen(index, odd, pick, cells, y_a, y_b, x_a, x_b, wide):
    even, core_0 = odd[0] == 0, odd[1] == 0
    for x in range(10):
        if x == 0:
            layer, side = jnp.where(core_0, x_b[index], x_a[index]).reshape(160, C), 0
        elif x == 9:
            layer, side = jnp.where(core_0, x_a[index], x_b[index]).reshape(160, C), 2
        else:
            a, b = y_a[index, x - 1], y_b[index, x - 1]
            layer = jnp.concatenate(
                [jnp.where(even, b, a), cells[x - 1].reshape(128, C), jnp.where(even, a, b)], axis=0
            )
            side = 1
        moved = jnp.dot(pick[side], layer, preferred_element_type=jnp.float32).astype(jnp.bfloat16)
        for oz in range(3):
            wide[oz, x] = moved[160 * oz : 160 * (oz + 1)].reshape(10, 16, C)


def widen_kernel(odd, pick, cells, y_a, y_b, x_a, x_b, wide):
    widen(0, odd, pick, cells, y_a, y_b, x_a, x_b, wide)


def part_kernel(member, where, wide, grad, own, coded, terms):
    g = grad[...].reshape(1024, C)
    for j in range(EACH):
        sides = []
        for side in range(2):
            k = jnp.minimum((where[2 + side] ^ member) * EACH + j, K - 1)
            lanes = pl.ds(pl.multiple_of((where[0] ^ side) * HALF, HALF), HALF)
            w = wide[k % 3, pl.ds(k // 9, 8), pl.ds((k // 3) % 3, 8), :, lanes]
            sides.append(w.reshape(1024, HALF))
        t = lax.dot_general(
            jnp.concatenate(sides, axis=1), g, (((0,), (0,)), ((), ())), preferred_element_type=jnp.float32
        )
        own[j * HALF : (j + 1) * HALF, :] = t[:HALF]
        terms[j * HALF : (j + 1) * HALF, :] = t[HALF:]
    for c in range(4):
        put_coded(lambda b, c=c: terms[c * ROWS + b * BLOCK : c * ROWS + (b + 1) * BLOCK, :], coded, c)


def convolve(back, wide, kernel, masks, out, sums):
    for x in range(0, 8, 2):
        total = None
        for k in range(K):
            ox, oy, oz = k // 9, (k // 3) % 3, k % 3
            if back:
                ox, oy, oz = 2 - ox, 2 - oy, 2 - oz
            w = wide[oz, ox + x : ox + x + 2, oy : oy + 8].reshape(256, C)
            d = lax.dot_general(
                w, kernel[k], (((1,), (1 if back else 0,)), ((), ())), preferred_element_type=jnp.float32
            )
            total = d if total is None else total + d
        sums[x * 128 : (x + 2) * 128, :] = total.astype(jnp.bfloat16)
    for x in range(8):
        cells = lax.dot_general(
            masks[x], sums[x * 128 : (x + 1) * 128, :], (((0,), (0,)), ((), ())),
            preferred_element_type=jnp.float32,
        ).astype(jnp.bfloat16)
        out[0, x] = cells[:64]
        out[1, x] = cells[64:]


def forward_kernel(wide, kernel, masks, out, sums):
    convolve(False, wide, kernel, masks, out, sums)


def backward_kernel(odd, pick, grad, y_a, y_b, x_a, x_b, kernel, masks, out, sums, wide):
    widen(1, odd, pick, grad, y_a, y_b, x_a, x_b, wide)
    convolve(True, wide, kernel, masks, out, sums)


def shards(features, cotangent, kernel, occupancy, neighbors):
    gx, gy = lax.axis_index("gx"), lax.axis_index("gy")
    core = gx % 2
    at = {"x": gy, "y": gx // 8, "z": (gx // 2) % 4}
    scale = 1.0 / (512.0 * 256.0) ** 0.5
    outer, inner = rank_in(0, core, at), rank_in(1, core, at)
    where = jnp.stack([core, inner, outer, rank_in(0, 1 - core, at), inner, rank_in(1, 1 - core, at)])
    where = where.astype(jnp.int32)

    odd = jnp.stack([gy % 2, core]).astype(jnp.int32)

    y_pairs = ([(0, 1), (1, 0), (2, 3), (3, 2)], [(1, 2), (2, 1)])
    x_pairs = ([(i, i ^ 1) for i in range(32)], [(i, i + 1 if i % 2 else i - 1) for i in range(1, 31)])

    column = shape((8, 8, 16, C), jnp.bfloat16)
    wide_shape = (3, 10, 10, 16, C)
    side_y = shape((2, 8, 16, C), jnp.bfloat16)
    side_x = shape((2, 10, 16, C), jnp.bfloat16)
    cells, grad, masks, *sides = call(
        prepare_kernel,
        [column, column, shape((8, 128, 128), jnp.bfloat16)] + [side_y] * 2,
        odd, features.reshape(2, 8, 64, C), cotangent.reshape(2, 8, 64, C), occupancy,
    )
    y_halo = [lax.ppermute(a, "gy", pairs) for a, pairs in zip(sides, y_pairs)]
    (pick,) = call(picks_kernel, [shape((3, 480, 160), jnp.bfloat16)], after(neighbors, sides[0]))
    edges = call(edges_kernel, [side_x, side_x], odd, cells, grad, *y_halo)
    x_halo = [lax.ppermute(a, "gx", pairs) for a, pairs in zip(edges, x_pairs)]
    (wide,) = call(widen_kernel, [shape(wide_shape, jnp.bfloat16)], odd, pick, cells, *y_halo, *x_halo)

    flops = 2 * K * 1024 * C * C
    sums = {}
    got = {}
    for m in (1, 2, 3, 0):
        own, coded = call(
            functools.partial(part_kernel, m),
            [shape((EACH * HALF, C), jnp.float32), CODED_4],
            where, wide, grad,
            flops=flops // 4,
            scratch=[pltpu.VMEM((EACH * HALF, C), jnp.float32)],
        )
        other = lax.ppermute(coded, BOTH, other_core())
        out = CODED_4 if m else shape((4, ROWS, C), jnp.float32)
        (sums[m],) = call(functools.partial(pair_sum_kernel, m == 0), [out], own, other)
        if m:
            got[m] = lax.ppermute(sums[m], BOTH, partners(0, m))

    brick_rows = shape((2, 8, 64, C), jnp.bfloat16)
    totals = pltpu.VMEM((1024, C), jnp.bfloat16)
    (forward,) = call(
        forward_kernel, [brick_rows], after(wide, sums[0], sums[3]), kernel, masks, flops=flops, scratch=[totals]
    )
    keep, *sent = call(
        group_sum_kernel,
        [shape((1, ROWS, C), jnp.float32)] + [CODED_1] * 3,
        inner.reshape(1).astype(jnp.int32), after(sums[0], forward), got[1], got[2], got[3],
    )
    (part,) = call(last_group_kernel, [CODED_1], keep, *exchange(sent, 1))
    (whole,) = call(total_kernel, [CODED_1], part, *exchange([part] * 3, 2))
    four = jnp.concatenate([whole] + exchange([whole] * 3, 1))
    sets = [four] + exchange([four] * 3, 0)
    (backward,) = call(
        backward_kernel, [brick_rows], odd, pick, after(grad, four), *y_halo, *x_halo, kernel, masks,
        flops=flops, scratch=[totals, pltpu.VMEM(wide_shape, jnp.bfloat16)],
    )
    others = [lax.ppermute(sets[0], BOTH, other_core())]
    done = finish(scale, where, [(0, 0), (1, 0)], [sets[0], others[0]], None)
    sets[1:] = [after(s, backward, done) for s in sets[1:]]
    others += [lax.ppermute(s, BOTH, other_core()) for s in sets[1:3]]
    done = finish(scale, where, [(0, 1), (0, 2)], sets[1:3], done)
    others.append(lax.ppermute(after(sets[3], done), BOTH, other_core()))
    done = finish(scale, where, [(0, 3), (1, 1), (1, 2)], [sets[3], *others[1:3]], done)
    done = finish(scale, where, [(1, 3)], others[3:], done)
    return forward.reshape(2, 8, 8, 8, C), backward.reshape(2, 8, 8, 8, C), done


def solution(mesh):
    placed = (
        P(BOTH, None, None, None, None),
        P(BOTH, None, None, None, None),
        P(),
        P(BOTH, None),
        P(BOTH, None),
    )
    return jax.shard_map(
        shards,
        mesh=mesh,
        in_specs=placed,
        out_specs=(P(BOTH, None, None, None, None), P(BOTH, None, None, None, None), P()),
        check_vma=False,
    )
```

```python
import functools

import jax
import jax.numpy as jnp
from jax import lax
from jax.experimental import pallas as pl
from jax.experimental.pallas import tpu as pltpu
from jax.sharding import PartitionSpec as P

BOTH = ("gx", "gy")
C = 256
HALF = 128
K = 27
EACH = 7
ROWS = 224
BLOCK = 32
BLOCKS = ROWS // BLOCK
CODED = ROWS + 16

CODED_4 = jax.ShapeDtypeStruct((4, CODED, C), jnp.int16)
CODED_1 = jax.ShapeDtypeStruct((1, CODED, C), jnp.int16)

VMEM = pl.BlockSpec(memory_space=pltpu.VMEM)
HBM = pl.BlockSpec(memory_space=pltpu.HBM)
SMEM = pl.BlockSpec(memory_space=pltpu.SMEM)
FREE = pl.CostEstimate(flops=0, bytes_accessed=0, transcendentals=0)
PARAMS = pltpu.CompilerParams(vmem_limit_bytes=28 * 2**20)

FIRST, SECOND = 0, 1
GROUPS = (
    ((("z", FIRST), ("y", SECOND)), (("x", FIRST), ("y", FIRST)), (("x", SECOND), ("z", SECOND))),
    ((("x", SECOND), ("y", FIRST)), (("x", FIRST), ("z", FIRST)), (("y", SECOND), ("z", SECOND))),
)


def paired(v, pairing):
    return v ^ 1 if pairing == FIRST else 3 - v


def pair_bit(v, pairing):
    return (v ^ (v >> 1)) & 1 if pairing == FIRST else v >> 1


def number(at):
    return ((at["y"] * 4 + at["z"]) * 2 + at["core"]) * 4 + at["x"]


def places():
    for y in range(4):
        for z in range(4):
            for core in range(2):
                for x in range(4):
                    yield {"x": x, "y": y, "z": z, "core": core}


def partners(level, member):
    pairs = []
    for at in places():
        to = dict(at)
        for i, (axis, pairing) in enumerate(GROUPS[at["core"]][level]):
            if member in ((1, 2), (1, 3))[i]:
                to[axis] = paired(to[axis], pairing)
        pairs.append((number(at), number(to)))
    return pairs


def other_core():
    return [(number(at), number({**at, "core": 1 - at["core"]})) for at in places()]


def rank_in(level, core, at):
    ranks = []
    for c in range(2):
        (a, pa), (b, pb) = GROUPS[c][level]
        u, v = pair_bit(at[a], pa), pair_bit(at[b], pb)
        ranks.append(2 * (u ^ v) + v)
    return jnp.where(core == 0, ranks[0], ranks[1])


def exchange(arrays, level, order=(1, 2, 3)):
    got = {m: lax.ppermute(arrays[m - 1], BOTH, partners(level, m)) for m in order}
    return [got[1], got[2], got[3]]


def after(value, *others):
    return lax.optimization_barrier((value, *others))[0]


def call(kernel, outs, *args, scratch=(), aliases=None):
    return pl.pallas_call(
        kernel,
        out_shape=list(outs),
        in_specs=[SMEM if a.dtype == jnp.int32 and a.size < 100 else VMEM for a in args],
        out_specs=[VMEM] * len(outs),
        scratch_shapes=list(scratch),
        input_output_aliases=aliases or {},
        compiler_params=PARAMS,
        cost_estimate=FREE,
    )(*args)


def shape(dims, dtype):
    return jax.ShapeDtypeStruct(dims, dtype)


def put_coded(read, ref, index):
    row = lax.broadcasted_iota(jnp.int32, (16, C), 0)
    exponents = jnp.zeros((16, C), jnp.float32)
    for b in range(BLOCKS):
        x = read(b)
        top = jnp.max(jnp.abs(x), axis=0, keepdims=True)
        e = jnp.ceil(jnp.log2(jnp.maximum(top, 2.0**-110)))
        q = jnp.clip(jnp.round(x * jnp.exp2(15.0 - e)), -32767.0, 32767.0)
        ref[index, b * BLOCK : (b + 1) * BLOCK, :] = q.astype(jnp.int16)
        exponents = jnp.where(row == b, e, exponents)
    ref[index, ROWS:CODED, :] = exponents.astype(jnp.int16)


def coded_scales(ref, index):
    return jnp.exp2(ref[index, ROWS:CODED, :].astype(jnp.float32) - 15.0)


def block_of(ref, index, b):
    return ref[index, b * BLOCK : (b + 1) * BLOCK, :]


def coded_block(ref, index, scales, b):
    return block_of(ref, index, b).astype(jnp.float32) * scales[b : b + 1, :]


def pair_sum_kernel(last, own, got, out):
    for c in range(4):
        scales = coded_scales(got, c)

        def read(b, c=c, scales=scales):
            rows = slice(c * ROWS + b * BLOCK, c * ROWS + (b + 1) * BLOCK)
            return own[rows, :] + coded_block(got, c, scales, b)

        if last:
            for b in range(BLOCKS):
                out[c, b * BLOCK : (b + 1) * BLOCK, :] = read(b)
        else:
            put_coded(read, out, c)


def group_sum_kernel(rank, own, got_1, got_2, got_3, keep, first, second, third):
    g = rank[0]
    for m, out in enumerate((keep, first, second, third)):
        at = g ^ m
        scales = [coded_scales(r, at) for r in (got_1, got_2, got_3)]

        def read(b, at=at, scales=scales):
            x = block_of(own, at, b)
            for r, s in zip((got_1, got_2, got_3), scales):
                x = x + coded_block(r, at, s, b)
            return x

        if m == 0:
            for b in range(BLOCKS):
                out[0, b * BLOCK : (b + 1) * BLOCK, :] = read(b)
        else:
            put_coded(read, out, 0)


def last_group_kernel(own, got_1, got_2, got_3, out):
    scales = [coded_scales(r, 0) for r in (got_1, got_2, got_3)]

    def read(b):
        x = block_of(own, 0, b)
        for r, s in zip((got_1, got_2, got_3), scales):
            x = x + coded_block(r, 0, s, b)
        return x

    put_coded(read, out, 0)


def total_kernel(own, got_1, got_2, got_3, out):
    refs = (own, got_1, got_2, got_3)
    scales = [coded_scales(r, 0) for r in refs]

    def read(b):
        a = [coded_block(r, 0, s, b) for r, s in zip(refs, scales)]
        return (a[0] + a[1]) + (a[2] + a[3])

    put_coded(read, out, 0)


def finish_kernel(scale, parts, where, *refs):
    n = len(parts)
    out, stage, done = refs[-3:]

    def copy_of(s, j):
        side, member = parts[s]
        k = (where[2 + side] ^ member) * EACH + j
        rows = pl.ds(pl.multiple_of((where[0] ^ side) * HALF, HALF), HALF)
        copy = pltpu.make_async_copy(stage.at[s, j], out.at[jnp.minimum(k, K - 1), rows, :], done.at[s, j])
        return k, copy

    def each(s, j, act):
        k, copy = copy_of(s, j)
        if j < EACH - 1:
            act(copy)
        else:
            pl.when(k < K)(lambda: act(copy))

    for s in range(n):
        for place in range(4):
            c = where[4 + parts[s][0]] ^ place
            scales = coded_scales(refs[s], c) * scale
            for b in range(BLOCKS):
                at = place * BLOCKS + b
                stage[s, at // 4, at % 4 * BLOCK : (at % 4 + 1) * BLOCK, :] = coded_block(refs[s], c, scales, b)
                if at % 4 == 3:
                    each(s, at // 4, lambda copy: copy.start())
    for s in range(n):
        for j in range(EACH):
            each(s, j, lambda copy: copy.wait())


def finish(scale, where, parts, sets, before):
    more = [] if before is None else [before]
    n = len(sets)
    return pl.pallas_call(
        functools.partial(finish_kernel, scale, parts),
        out_shape=shape((K, C, C), jnp.float32),
        in_specs=[SMEM] + [VMEM] * n + [HBM] * len(more),
        out_specs=HBM,
        scratch_shapes=[pltpu.VMEM((n, EACH, HALF, C), jnp.float32), pltpu.SemaphoreType.DMA((n, EACH))],
        input_output_aliases={1 + n: 0} if more else {},
        compiler_params=PARAMS,
        cost_estimate=FREE,
    )(where, *sets, *more)


def prepare_kernel(odd, features, cotangent, occupancy, cells, grad, masks, x_a, x_b, y_a, y_b):
    r = lax.broadcasted_iota(jnp.int32, (128, 128), 0)
    c = lax.broadcasted_iota(jnp.int32, (128, 128), 1)
    same = (r >> 4 == (c >> 3) & 7) & ((r >> 3) & 1 == c >> 6) & (r & 7 == c & 7)
    low = lax.broadcasted_iota(jnp.int32, (1, 128), 1) < 64
    occupied = occupancy[...].astype(jnp.float32)
    turned = pltpu.roll(occupied, 64, 1)
    even, core_0 = odd[0] == 0, odd[1] == 0
    ends = {}
    for x in range(8):
        lanes = slice(128 * (x // 2), 128 * (x // 2) + 128)
        if x % 2 == 0:
            row = jnp.where(low, occupied[0:1, lanes], turned[1:2, lanes])
        else:
            after_it = slice((lanes.start + 128) % 512, (lanes.start + 128) % 512 + 128)
            row = jnp.where(low, turned[0:1, after_it], occupied[1:2, lanes])
        pick = jnp.where(same, row, 0.0).astype(jnp.bfloat16)
        masks[x] = pick
        for index, (source, out) in enumerate(((features, cells), (cotangent, grad))):
            layer = jnp.concatenate([source[0, x], source[1, x]], axis=0)
            made = jnp.dot(pick, layer, preferred_element_type=jnp.float32).astype(jnp.bfloat16)
            made = made.reshape(8, 16, C)
            out[x] = made
            y_a[index, x] = jnp.where(even, made[7], made[0])
            y_b[index, x] = jnp.where(even, made[0], made[7])
            ends[index, x] = made
    for index in range(2):
        x_a[index] = jnp.where(core_0, ends[index, 7], ends[index, 0])
        x_b[index] = jnp.where(core_0, ends[index, 0], ends[index, 7])


def picks_kernel(neighbors, out):
    r = lax.broadcasted_iota(jnp.int32, (160, 160), 0)
    c = lax.broadcasted_iota(jnp.int32, (160, 160), 1)
    y, s, z = r >> 4, (r >> 3) & 1, r & 7
    same = y == c >> 4
    side_y = jnp.where(y == 0, 0, jnp.where(y == 9, 2, 1))
    which = side_y * 2 + s
    for ox in range(3):
        for oz in range(3):
            edge = z == (0 if oz == 0 else 7)
            slot = jnp.full((160, 160), -1, jnp.int32)
            for oy in range(3):
                for brick in range(2):
                    level = neighbors[brick, 9 * ox + 3 * oy + 1]
                    beyond = neighbors[brick, 9 * ox + 3 * oy + oz]
                    found = jnp.where(edge, beyond, level) if oz != 1 else level
                    slot = jnp.where(which == 2 * oy + brick, found, slot)
            hit = same & (slot >= 0) & ((c & 15) == slot * 8 + ((z + oz - 1) & 7))
            out[ox, 160 * oz : 160 * (oz + 1), :] = jnp.where(hit, 1.0, 0.0).astype(jnp.bfloat16)


def corners_kernel(odd, x_a, x_b, c_a, c_b):
    even = odd[0] == 0
    for side, x in enumerate((x_a, x_b)):
        for index in range(2):
            c_a[side, index] = jnp.where(even, x[index, 7], x[index, 0])
            c_b[side, index] = jnp.where(even, x[index, 0], x[index, 7])


def spread(pick, layer, x, wide):
    moved = jnp.dot(pick, layer, preferred_element_type=jnp.float32).astype(jnp.bfloat16)
    for oz in range(3):
        wide[oz, x] = moved[160 * oz : 160 * (oz + 1)].reshape(10, 16, C)


def widen_inner(index, odd, pick, cells, y_a, y_b, wide):
    even = odd[0] == 0
    for x in range(8):
        a, b = y_a[index, x], y_b[index, x]
        layer = [jnp.where(even, b, a), cells[x].reshape(128, C), jnp.where(even, a, b)]
        spread(pick[1], jnp.concatenate(layer, axis=0), x + 1, wide)


def widen_outer(index, odd, pick, x_a, x_b, c_a, c_b, wide):
    even, core_0 = odd[0] == 0, odd[1] == 0
    layers = []
    for side, x in enumerate((x_a, x_b)):
        a, b = c_a[side, index], c_b[side, index]
        rows = [jnp.where(even, b, a), x[index].reshape(128, C), jnp.where(even, a, b)]
        layers.append(jnp.concatenate(rows, axis=0))
    spread(pick[0], jnp.where(core_0, layers[1], layers[0]), 0, wide)
    spread(pick[2], jnp.where(core_0, layers[0], layers[1]), 9, wide)


def inner_kernel(odd, pick, cells, y_a, y_b, wide):
    widen_inner(0, odd, pick, cells, y_a, y_b, wide)


def outer_kernel(odd, pick, x_a, x_b, c_a, c_b, _, wide):
    widen_outer(0, odd, pick, x_a, x_b, c_a, c_b, wide)


def part_kernel(member, where, wide, grad, own, coded, terms):
    g = grad[...].reshape(1024, C)
    for j in range(EACH):
        sides = []
        for side in range(2):
            k = jnp.minimum((where[2 + side] ^ member) * EACH + j, K - 1)
            lanes = pl.ds(pl.multiple_of((where[0] ^ side) * HALF, HALF), HALF)
            w = wide[k % 3, pl.ds(k // 9, 8), pl.ds((k // 3) % 3, 8), :, lanes]
            sides.append(w.reshape(1024, HALF))
        t = lax.dot_general(
            jnp.concatenate(sides, axis=1), g, (((0,), (0,)), ((), ())), preferred_element_type=jnp.float32
        )
        own[j * HALF : (j + 1) * HALF, :] = t[:HALF]
        terms[j * HALF : (j + 1) * HALF, :] = t[HALF:]
    for c in range(4):
        put_coded(lambda b, c=c: terms[c * ROWS + b * BLOCK : c * ROWS + (b + 1) * BLOCK, :], coded, c)


def convolve(back, wide, kernel, masks, out, sums):
    for x in range(0, 8, 2):
        total = None
        for k in range(K):
            ox, oy, oz = k // 9, (k // 3) % 3, k % 3
            if back:
                ox, oy, oz = 2 - ox, 2 - oy, 2 - oz
            w = wide[oz, ox + x : ox + x + 2, oy : oy + 8].reshape(256, C)
            d = lax.dot_general(
                w, kernel[k], (((1,), (1 if back else 0,)), ((), ())), preferred_element_type=jnp.float32
            )
            total = d if total is None else total + d
        sums[x * 128 : (x + 2) * 128, :] = total.astype(jnp.bfloat16)
    for x in range(8):
        cells = lax.dot_general(
            masks[x], sums[x * 128 : (x + 1) * 128, :], (((0,), (0,)), ((), ())),
            preferred_element_type=jnp.float32,
        ).astype(jnp.bfloat16)
        out[0, x] = cells[:64]
        out[1, x] = cells[64:]


def forward_kernel(wide, kernel, masks, out, sums):
    convolve(False, wide, kernel, masks, out, sums)


def backward_kernel(odd, pick, grad, y_a, y_b, x_a, x_b, c_a, c_b, kernel, masks, out, sums, wide):
    widen_inner(1, odd, pick, grad, y_a, y_b, wide)
    widen_outer(1, odd, pick, x_a, x_b, c_a, c_b, wide)
    convolve(True, wide, kernel, masks, out, sums)


def shards(features, cotangent, kernel, occupancy, neighbors):
    gx, gy = lax.axis_index("gx"), lax.axis_index("gy")
    core = gx % 2
    at = {"x": gy, "y": gx // 8, "z": (gx // 2) % 4}
    scale = 1.0 / (512.0 * 256.0) ** 0.5
    outer, inner = rank_in(0, core, at), rank_in(1, core, at)
    where = jnp.stack([core, inner, outer, rank_in(0, 1 - core, at), inner, rank_in(1, 1 - core, at)])
    where = where.astype(jnp.int32)

    odd = jnp.stack([gy % 2, core]).astype(jnp.int32)

    y_pairs = ([(0, 1), (1, 0), (2, 3), (3, 2)], [(1, 2), (2, 1)])
    x_pairs = ([(i, i ^ 1) for i in range(32)], [(i, i + 1 if i % 2 else i - 1) for i in range(1, 31)])

    column = shape((8, 8, 16, C), jnp.bfloat16)
    wide_shape = (3, 10, 10, 16, C)
    side = shape((2, 8, 16, C), jnp.bfloat16)
    corner = shape((2, 2, 16, C), jnp.bfloat16)

    def swap(arrays, axis, pairs):
        return [lax.ppermute(a, axis, p) for a, p in zip(arrays, pairs)]

    cells, grad, masks, x_a, x_b, y_a, y_b = call(
        prepare_kernel,
        [column, column, shape((8, 128, 128), jnp.bfloat16)] + [side] * 4,
        odd, features.reshape(2, 8, 64, C), cotangent.reshape(2, 8, 64, C), occupancy,
    )
    x_halo = swap((x_a, x_b), "gx", x_pairs)
    y_halo = swap((after(y_a, x_halo[0]), after(y_b, x_halo[0])), "gy", y_pairs)
    (pick,) = call(picks_kernel, [shape((3, 480, 160), jnp.bfloat16)], after(neighbors, x_halo[0]))
    corners = swap(call(corners_kernel, [corner, corner], odd, *x_halo), "gy", y_pairs)
    (wide,) = call(inner_kernel, [shape(wide_shape, jnp.bfloat16)], odd, pick, cells, *y_halo)
    halo = (*x_halo, *corners)
    (wide,) = call(outer_kernel, [shape(wide_shape, jnp.bfloat16)], odd, pick, *halo, wide, aliases={6: 0})

    sums = {}
    got = {}
    before = []
    for m in (1, 2, 3, 0):
        own, coded = call(
            functools.partial(part_kernel, m),
            [shape((EACH * HALF, C), jnp.float32), CODED_4],
            where, after(wide, *before), grad,
            scratch=[pltpu.VMEM((EACH * HALF, C), jnp.float32)],
        )
        other = lax.ppermute(coded, BOTH, other_core())
        out = CODED_4 if m else shape((4, ROWS, C), jnp.float32)
        (sums[m],) = call(functools.partial(pair_sum_kernel, m == 0), [out], own, other)
        before = [own] + list(sums.values())[-2:-1]
        if m:
            got[m] = lax.ppermute(sums[m], BOTH, partners(0, m))

    brick_rows = shape((2, 8, 64, C), jnp.bfloat16)
    totals = pltpu.VMEM((1024, C), jnp.bfloat16)
    (forward,) = call(
        forward_kernel, [brick_rows], after(wide, sums[0], sums[3]), kernel, masks, scratch=[totals]
    )
    (backward,) = call(
        backward_kernel, [brick_rows], odd, pick, after(grad, forward), *y_halo, *halo, kernel, masks,
        scratch=[totals, pltpu.VMEM(wide_shape, jnp.bfloat16)],
    )
    keep, *sent = call(
        group_sum_kernel,
        [shape((1, ROWS, C), jnp.float32)] + [CODED_1] * 3,
        inner.reshape(1).astype(jnp.int32), after(sums[0], backward), got[1], got[2], got[3],
    )
    (part,) = call(last_group_kernel, [CODED_1], keep, *exchange(sent, 1))
    (whole,) = call(total_kernel, [CODED_1], part, *exchange([part] * 3, 2, (2, 3, 1)))
    four = jnp.concatenate([whole] + exchange([whole] * 3, 1, (2, 3, 1)))
    sets = [four] + exchange([four] * 3, 0)

    def other(a):
        return lax.ppermute(a, BOTH, other_core())

    done = finish(scale, where, [(0, 0)], [four], None)
    *own, done = lax.optimization_barrier((*sets, done))
    far = [other(a) for a in own]
    done = finish(scale, where, [(0, 1), (0, 2), (0, 3)], own[1:], done)
    done = finish(scale, where, [(1, 0), (1, 1), (1, 2), (1, 3)], far, done)
    return forward.reshape(2, 8, 8, 8, C), backward.reshape(2, 8, 8, 8, C), done


def solution(mesh):
    placed = (
        P(BOTH, None, None, None, None),
        P(BOTH, None, None, None, None),
        P(),
        P(BOTH, None),
        P(BOTH, None),
    )
    return jax.shard_map(
        shards,
        mesh=mesh,
        in_specs=placed,
        out_specs=(P(BOTH, None, None, None, None), P(BOTH, None, None, None, None), P()),
        check_vma=False,
    )
```

```python
import functools

import jax
import jax.numpy as jnp
from jax import lax
from jax.experimental import pallas as pl
from jax.experimental.pallas import tpu as pltpu
from jax.sharding import PartitionSpec as P

BOTH = ("gx", "gy")
C = 256
HALF = 128
K = 27
EACH = 7
ROWS = 224
BLOCK = 32
BLOCKS = ROWS // BLOCK
CODED = ROWS + 16

CODED_4 = jax.ShapeDtypeStruct((4, CODED, C), jnp.int16)
CODED_1 = jax.ShapeDtypeStruct((1, CODED, C), jnp.int16)

VMEM = pl.BlockSpec(memory_space=pltpu.VMEM)
HBM = pl.BlockSpec(memory_space=pltpu.HBM)
SMEM = pl.BlockSpec(memory_space=pltpu.SMEM)
FREE = pl.CostEstimate(flops=0, bytes_accessed=0, transcendentals=0)
PARAMS = pltpu.CompilerParams(vmem_limit_bytes=28 * 2**20)

FIRST, SECOND = 0, 1
GROUPS = (
    ((("z", FIRST), ("x", SECOND)), (("x", FIRST), ("y", FIRST)), (("y", SECOND), ("z", SECOND))),
    ((("y", SECOND), ("z", SECOND)), (("x", FIRST), ("y", FIRST)), (("z", FIRST), ("x", SECOND))),
)


def paired(v, pairing):
    return v ^ 1 if pairing == FIRST else 3 - v


def pair_bit(v, pairing):
    return (v ^ (v >> 1)) & 1 if pairing == FIRST else v >> 1


def number(at):
    return ((at["y"] * 4 + at["z"]) * 2 + at["core"]) * 4 + at["x"]


def places():
    for y in range(4):
        for z in range(4):
            for core in range(2):
                for x in range(4):
                    yield {"x": x, "y": y, "z": z, "core": core}


def partners(level, member):
    pairs = []
    for at in places():
        to = dict(at)
        for i, (axis, pairing) in enumerate(GROUPS[at["core"]][level]):
            if member in ((1, 2), (1, 3))[i]:
                to[axis] = paired(to[axis], pairing)
        pairs.append((number(at), number(to)))
    return pairs


def other_core():
    return [(number(at), number({**at, "core": 1 - at["core"]})) for at in places()]


def rank_in(level, core, at):
    ranks = []
    for c in range(2):
        (a, pa), (b, pb) = GROUPS[c][level]
        u, v = pair_bit(at[a], pa), pair_bit(at[b], pb)
        ranks.append(2 * (u ^ v) + v)
    return jnp.where(core == 0, ranks[0], ranks[1])


def exchange(arrays, level, order=(1, 2, 3)):
    got = {m: lax.ppermute(arrays[m - 1], BOTH, partners(level, m)) for m in order}
    return [got[1], got[2], got[3]]


def after(value, *others):
    return lax.optimization_barrier((value, *others))[0]


def call(kernel, outs, *args, scratch=(), aliases=None, cost=FREE):
    return pl.pallas_call(
        kernel,
        out_shape=list(outs),
        in_specs=[SMEM if a.dtype == jnp.int32 and a.size < 100 else VMEM for a in args],
        out_specs=[VMEM] * len(outs),
        scratch_shapes=list(scratch),
        input_output_aliases=aliases or {},
        compiler_params=PARAMS,
        cost_estimate=cost,
    )(*args)


def shape(dims, dtype):
    return jax.ShapeDtypeStruct(dims, dtype)


def put_coded(read, ref, index):
    row = lax.broadcasted_iota(jnp.int32, (16, C), 0)
    exponents = jnp.zeros((16, C), jnp.float32)
    for b in range(BLOCKS):
        x = read(b)
        top = jnp.max(jnp.abs(x), axis=0, keepdims=True)
        e = jnp.ceil(jnp.log2(jnp.maximum(top, 2.0**-110)))
        q = jnp.clip(jnp.round(x * jnp.exp2(15.0 - e)), -32767.0, 32767.0)
        ref[index, b * BLOCK : (b + 1) * BLOCK, :] = q.astype(jnp.int16)
        exponents = jnp.where(row == b, e, exponents)
    ref[index, ROWS:CODED, :] = exponents.astype(jnp.int16)


def coded_scales(ref, index):
    return jnp.exp2(ref[index, ROWS:CODED, :].astype(jnp.float32) - 15.0)


def block_of(ref, index, b):
    return ref[index, b * BLOCK : (b + 1) * BLOCK, :]


def coded_block(ref, index, scales, b):
    return block_of(ref, index, b).astype(jnp.float32) * scales[b : b + 1, :]


def pair_sum_kernel(last, own, got, out):
    for c in range(4):
        scales = coded_scales(got, c)

        def read(b, c=c, scales=scales):
            rows = slice(c * ROWS + b * BLOCK, c * ROWS + (b + 1) * BLOCK)
            return own[rows, :] + coded_block(got, c, scales, b)

        if last:
            for b in range(BLOCKS):
                out[c, b * BLOCK : (b + 1) * BLOCK, :] = read(b)
        else:
            put_coded(read, out, c)


def group_sum_kernel(rank, own, got_1, got_2, got_3, keep, first, second, third):
    g = rank[0]
    for m, out in enumerate((keep, first, second, third)):
        at = g ^ m
        scales = [coded_scales(r, at) for r in (got_1, got_2, got_3)]

        def read(b, at=at, scales=scales):
            x = block_of(own, at, b)
            for r, s in zip((got_1, got_2, got_3), scales):
                x = x + coded_block(r, at, s, b)
            return x

        if m == 0:
            for b in range(BLOCKS):
                out[0, b * BLOCK : (b + 1) * BLOCK, :] = read(b)
        else:
            put_coded(read, out, 0)


def last_group_kernel(own, got_1, got_2, got_3, out):
    scales = [coded_scales(r, 0) for r in (got_1, got_2, got_3)]

    def read(b):
        x = block_of(own, 0, b)
        for r, s in zip((got_1, got_2, got_3), scales):
            x = x + coded_block(r, 0, s, b)
        return x

    put_coded(read, out, 0)


def total_kernel(own, got_1, got_2, got_3, out):
    refs = (own, got_1, got_2, got_3)
    scales = [coded_scales(r, 0) for r in refs]

    def read(b):
        a = [coded_block(r, 0, s, b) for r, s in zip(refs, scales)]
        return (a[0] + a[1]) + (a[2] + a[3])

    put_coded(read, out, 0)


def finish_kernel(scale, parts, where, *refs):
    n = len(parts)
    out, stage, done = refs[-3:]

    def copy_of(s, j):
        side, member = parts[s]
        k = (where[2 + side] ^ member) * EACH + j
        rows = pl.ds(pl.multiple_of((where[0] ^ side) * HALF, HALF), HALF)
        copy = pltpu.make_async_copy(stage.at[s, j], out.at[jnp.minimum(k, K - 1), rows, :], done.at[s, j])
        return k, copy

    def each(s, j, act):
        k, copy = copy_of(s, j)
        if j < EACH - 1:
            act(copy)
        else:
            pl.when(k < K)(lambda: act(copy))

    for s in range(n):
        for place in range(4):
            c = where[4 + parts[s][0]] ^ place
            scales = coded_scales(refs[s], c) * scale
            for b in range(BLOCKS):
                at = place * BLOCKS + b
                stage[s, at // 4, at % 4 * BLOCK : (at % 4 + 1) * BLOCK, :] = coded_block(refs[s], c, scales, b)
                if at % 4 == 3:
                    each(s, at // 4, lambda copy: copy.start())
    for s in range(n):
        for j in range(EACH):
            each(s, j, lambda copy: copy.wait())


def finish(scale, where, parts, sets, before):
    more = [] if before is None else [before]
    n = len(sets)
    return pl.pallas_call(
        functools.partial(finish_kernel, scale, parts),
        out_shape=shape((K, C, C), jnp.float32),
        in_specs=[SMEM] + [VMEM] * n + [HBM] * len(more),
        out_specs=HBM,
        scratch_shapes=[pltpu.VMEM((n, EACH, HALF, C), jnp.float32), pltpu.SemaphoreType.DMA((n, EACH))],
        input_output_aliases={1 + n: 0} if more else {},
        compiler_params=PARAMS,
        cost_estimate=FREE,
    )(where, *sets, *more)


def prepare_kernel(odd, features, cotangent, occupancy, cells, grad, masks, x_a, x_b, y_a, y_b):
    r = lax.broadcasted_iota(jnp.int32, (128, 128), 0)
    c = lax.broadcasted_iota(jnp.int32, (128, 128), 1)
    same = (r >> 4 == (c >> 3) & 7) & ((r >> 3) & 1 == c >> 6) & (r & 7 == c & 7)
    low = lax.broadcasted_iota(jnp.int32, (1, 128), 1) < 64
    occupied = occupancy[...].astype(jnp.float32)
    turned = pltpu.roll(occupied, 64, 1)
    even, core_0 = odd[0] == 0, odd[1] == 0
    ends = {}
    for x in range(8):
        lanes = slice(128 * (x // 2), 128 * (x // 2) + 128)
        if x % 2 == 0:
            row = jnp.where(low, occupied[0:1, lanes], turned[1:2, lanes])
        else:
            after_it = slice((lanes.start + 128) % 512, (lanes.start + 128) % 512 + 128)
            row = jnp.where(low, turned[0:1, after_it], occupied[1:2, lanes])
        pick = jnp.where(same, row, 0.0).astype(jnp.bfloat16)
        masks[x] = pick
        for index, (source, out) in enumerate(((features, cells), (cotangent, grad))):
            layer = jnp.concatenate([source[0, x], source[1, x]], axis=0)
            made = jnp.dot(pick, layer, preferred_element_type=jnp.float32).astype(jnp.bfloat16)
            made = made.reshape(8, 16, C)
            out[x] = made
            y_a[index, x] = jnp.where(even, made[7], made[0])
            y_b[index, x] = jnp.where(even, made[0], made[7])
            ends[index, x] = made
    for index in range(2):
        x_a[index] = jnp.where(core_0, ends[index, 7], ends[index, 0])
        x_b[index] = jnp.where(core_0, ends[index, 0], ends[index, 7])


def picks_kernel(neighbors, out):
    r = lax.broadcasted_iota(jnp.int32, (160, 160), 0)
    c = lax.broadcasted_iota(jnp.int32, (160, 160), 1)
    y, s, z = r >> 4, (r >> 3) & 1, r & 7
    same = y == c >> 4
    side_y = jnp.where(y == 0, 0, jnp.where(y == 9, 2, 1))
    which = side_y * 2 + s
    for ox in range(3):
        for oz in range(3):
            edge = z == (0 if oz == 0 else 7)
            slot = jnp.full((160, 160), -1, jnp.int32)
            for oy in range(3):
                for brick in range(2):
                    level = neighbors[brick, 9 * ox + 3 * oy + 1]
                    beyond = neighbors[brick, 9 * ox + 3 * oy + oz]
                    found = jnp.where(edge, beyond, level) if oz != 1 else level
                    slot = jnp.where(which == 2 * oy + brick, found, slot)
            hit = same & (slot >= 0) & ((c & 15) == slot * 8 + ((z + oz - 1) & 7))
            out[ox, 160 * oz : 160 * (oz + 1), :] = jnp.where(hit, 1.0, 0.0).astype(jnp.bfloat16)


def corners_kernel(odd, x_a, x_b, c_a, c_b):
    even = odd[0] == 0
    for side, x in enumerate((x_a, x_b)):
        for index in range(2):
            c_a[side, index] = jnp.where(even, x[index, 7], x[index, 0])
            c_b[side, index] = jnp.where(even, x[index, 0], x[index, 7])


def spread(pick, layer, x, wide):
    moved = jnp.dot(pick, layer, preferred_element_type=jnp.float32).astype(jnp.bfloat16)
    for oz in range(3):
        wide[oz, x] = moved[160 * oz : 160 * (oz + 1)].reshape(10, 16, C)


def widen_inner(index, odd, pick, cells, y_a, y_b, wide):
    even = odd[0] == 0
    for x in range(8):
        a, b = y_a[index, x], y_b[index, x]
        layer = [jnp.where(even, b, a), cells[x].reshape(128, C), jnp.where(even, a, b)]
        spread(pick[1], jnp.concatenate(layer, axis=0), x + 1, wide)


def widen_outer(index, odd, pick, x_a, x_b, c_a, c_b, wide):
    even, core_0 = odd[0] == 0, odd[1] == 0
    layers = []
    for side, x in enumerate((x_a, x_b)):
        a, b = c_a[side, index], c_b[side, index]
        rows = [jnp.where(even, b, a), x[index].reshape(128, C), jnp.where(even, a, b)]
        layers.append(jnp.concatenate(rows, axis=0))
    spread(pick[0], jnp.where(core_0, layers[1], layers[0]), 0, wide)
    spread(pick[2], jnp.where(core_0, layers[0], layers[1]), 9, wide)


def inner_kernel(odd, pick, cells, y_a, y_b, wide):
    widen_inner(0, odd, pick, cells, y_a, y_b, wide)


def outer_kernel(odd, pick, x_a, x_b, c_a, c_b, _, wide):
    widen_outer(0, odd, pick, x_a, x_b, c_a, c_b, wide)


def part_kernel(member, where, wide, grad, own, coded, terms):
    g = grad[...].reshape(1024, C)
    for j in range(EACH):
        sides = []
        for side in range(2):
            k = jnp.minimum((where[2 + side] ^ member) * EACH + j, K - 1)
            lanes = pl.ds(pl.multiple_of((where[0] ^ side) * HALF, HALF), HALF)
            w = wide[k % 3, pl.ds(k // 9, 8), pl.ds((k // 3) % 3, 8), :, lanes]
            sides.append(w.reshape(1024, HALF))
        t = lax.dot_general(
            jnp.concatenate(sides, axis=1), g, (((0,), (0,)), ((), ())), preferred_element_type=jnp.float32
        )
        own[j * HALF : (j + 1) * HALF, :] = t[:HALF]
        terms[j * HALF : (j + 1) * HALF, :] = t[HALF:]
    for c in range(4):
        put_coded(lambda b, c=c: terms[c * ROWS + b * BLOCK : c * ROWS + (b + 1) * BLOCK, :], coded, c)


def convolve(back, wide, kernel, masks, out, sums):
    for x in range(0, 8, 2):
        total = None
        for k in range(K):
            ox, oy, oz = k // 9, (k // 3) % 3, k % 3
            if back:
                ox, oy, oz = 2 - ox, 2 - oy, 2 - oz
            w = wide[oz, ox + x : ox + x + 2, oy : oy + 8].reshape(256, C)
            d = lax.dot_general(
                w, kernel[k], (((1,), (1 if back else 0,)), ((), ())), preferred_element_type=jnp.float32
            )
            total = d if total is None else total + d
        sums[x * 128 : (x + 2) * 128, :] = total.astype(jnp.bfloat16)
    for x in range(8):
        cells = lax.dot_general(
            masks[x], sums[x * 128 : (x + 1) * 128, :], (((0,), (0,)), ((), ())),
            preferred_element_type=jnp.float32,
        ).astype(jnp.bfloat16)
        out[0, x] = cells[:64]
        out[1, x] = cells[64:]


def forward_kernel(wide, kernel, masks, out, sums):
    convolve(False, wide, kernel, masks, out, sums)


def backward_kernel(odd, pick, grad, y_a, y_b, x_a, x_b, c_a, c_b, kernel, masks, out, sums, wide):
    widen_inner(1, odd, pick, grad, y_a, y_b, wide)
    widen_outer(1, odd, pick, x_a, x_b, c_a, c_b, wide)
    convolve(True, wide, kernel, masks, out, sums)


def shards(features, cotangent, kernel, occupancy, neighbors):
    gx, gy = lax.axis_index("gx"), lax.axis_index("gy")
    core = gx % 2
    at = {"x": gy, "y": gx // 8, "z": (gx // 2) % 4}
    scale = 1.0 / (512.0 * 256.0) ** 0.5
    outer, inner = rank_in(0, core, at), rank_in(1, core, at)
    where = jnp.stack([core, inner, outer, rank_in(0, 1 - core, at), inner, rank_in(1, 1 - core, at)])
    where = where.astype(jnp.int32)

    odd = jnp.stack([gy % 2, core]).astype(jnp.int32)

    y_pairs = ([(0, 1), (1, 0), (2, 3), (3, 2)], [(1, 2), (2, 1)])
    x_pairs = ([(i, i ^ 1) for i in range(32)], [(i, i + 1 if i % 2 else i - 1) for i in range(1, 31)])

    column = shape((8, 8, 16, C), jnp.bfloat16)
    wide_shape = (3, 10, 10, 16, C)
    side = shape((2, 8, 16, C), jnp.bfloat16)
    corner = shape((2, 2, 16, C), jnp.bfloat16)

    def swap(arrays, axis, pairs):
        return [lax.ppermute(a, axis, p) for a, p in zip(arrays, pairs)]

    busy = pl.CostEstimate(flops=2**31, bytes_accessed=2**22, transcendentals=0)
    (pick,) = call(picks_kernel, [shape((3, 480, 160), jnp.bfloat16)], neighbors, cost=busy)
    odd = after(odd, pick)
    cells, grad, masks, x_a, x_b, y_a, y_b = call(
        prepare_kernel,
        [column, column, shape((8, 128, 128), jnp.bfloat16)] + [side] * 4,
        odd, features.reshape(2, 8, 64, C), cotangent.reshape(2, 8, 64, C), occupancy,
    )
    x_halo = swap((x_a, x_b), "gx", x_pairs)
    y_halo = swap((after(y_a, x_halo[0]), after(y_b, x_halo[0])), "gy", y_pairs)
    corners = swap(call(corners_kernel, [corner, corner], odd, *x_halo), "gy", y_pairs)
    (wide,) = call(inner_kernel, [shape(wide_shape, jnp.bfloat16)], odd, pick, cells, *y_halo)
    halo = (*x_halo, *corners)
    (wide,) = call(outer_kernel, [shape(wide_shape, jnp.bfloat16)], odd, pick, *halo, wide, aliases={6: 0})

    sums, got, before = {}, {}, []

    def part(m, *before):
        return call(
            functools.partial(part_kernel, m),
            [shape((EACH * HALF, C), jnp.float32), CODED_4],
            where, after(wide, *before), grad,
            scratch=[pltpu.VMEM((EACH * HALF, C), jnp.float32)],
        )

    def chip_sum(m, own, got):
        out = CODED_4 if m else shape((4, ROWS, C), jnp.float32)
        return call(functools.partial(pair_sum_kernel, m == 0), [out], own, got)[0]

    for m in (0, 1, 2, 3):
        own, coded = part(m, *before)
        sums[m] = chip_sum(m, own, lax.ppermute(coded, BOTH, other_core()))
        before = [own] + list(sums.values())[-2:-1]
        if m:
            got[m] = lax.ppermute(sums[m], BOTH, partners(0, m))
    brick_rows = shape((2, 8, 64, C), jnp.bfloat16)
    totals = pltpu.VMEM((1024, C), jnp.bfloat16)
    (forward,) = call(forward_kernel, [brick_rows], after(wide, sums[3]), kernel, masks, scratch=[totals])
    keep, *sent = call(
        group_sum_kernel,
        [shape((1, ROWS, C), jnp.float32)] + [CODED_1] * 3,
        inner.reshape(1).astype(jnp.int32), after(sums[0], forward), got[1], got[2], got[3],
    )
    (partial,) = call(last_group_kernel, [CODED_1], keep, *exchange(sent, 1))
    (whole,) = call(total_kernel, [CODED_1], partial, *exchange([partial] * 3, 2, (2, 3, 1)))
    four = jnp.concatenate([whole] + exchange([whole] * 3, 1, (2, 3, 1)))
    sets = [four] + exchange([four] * 3, 0)

    (backward,) = call(
        backward_kernel, [brick_rows], odd, pick, after(grad, four), *y_halo, *halo, kernel, masks,
        scratch=[totals, pltpu.VMEM(wide_shape, jnp.bfloat16)],
    )

    def other(a):
        return lax.ppermute(a, BOTH, other_core())

    done = finish(scale, where, [(0, 0)], [after(four, backward)], None)
    *own, done = lax.optimization_barrier((*sets, done))
    far = [other(a) for a in own]
    done = finish(scale, where, [(0, 1), (0, 2), (0, 3)], own[1:], done)
    done = finish(scale, where, [(1, 0), (1, 1), (1, 2), (1, 3)], far, done)
    return forward.reshape(2, 8, 8, 8, C), backward.reshape(2, 8, 8, 8, C), done


def solution(mesh):
    placed = (
        P(BOTH, None, None, None, None),
        P(BOTH, None, None, None, None),
        P(),
        P(BOTH, None),
        P(BOTH, None),
    )
    return jax.shard_map(
        shards,
        mesh=mesh,
        in_specs=placed,
        out_specs=(P(BOTH, None, None, None, None), P(BOTH, None, None, None, None), P()),
        check_vma=False,
    )
```

```python
import functools

import jax
import jax.numpy as jnp
from jax import lax
from jax.experimental import pallas as pl
from jax.experimental.pallas import tpu as pltpu
from jax.sharding import PartitionSpec as P

BOTH = ("gx", "gy")
C = 256
HALF = 128
K = 27
EACH = 7
ROWS = 224
BLOCK = 32
BLOCKS = ROWS // BLOCK
CODED = ROWS + 16

CODED_4 = jax.ShapeDtypeStruct((4, CODED, C), jnp.int16)
CODED_1 = jax.ShapeDtypeStruct((1, CODED, C), jnp.int16)

VMEM = pl.BlockSpec(memory_space=pltpu.VMEM)
HBM = pl.BlockSpec(memory_space=pltpu.HBM)
SMEM = pl.BlockSpec(memory_space=pltpu.SMEM)
FREE = pl.CostEstimate(flops=0, bytes_accessed=0, transcendentals=0)
PARAMS = pltpu.CompilerParams(vmem_limit_bytes=28 * 2**20)

FIRST, SECOND = 0, 1
GROUPS = (
    ((("z", FIRST), ("x", SECOND)), (("x", FIRST), ("y", FIRST)), (("y", SECOND), ("z", SECOND))),
    ((("y", SECOND), ("z", SECOND)), (("x", FIRST), ("y", FIRST)), (("z", FIRST), ("x", SECOND))),
)


def paired(v, pairing):
    return v ^ 1 if pairing == FIRST else 3 - v


def pair_bit(v, pairing):
    return (v ^ (v >> 1)) & 1 if pairing == FIRST else v >> 1


def number(at):
    return ((at["y"] * 4 + at["z"]) * 2 + at["core"]) * 4 + at["x"]


def places():
    for y in range(4):
        for z in range(4):
            for core in range(2):
                for x in range(4):
                    yield {"x": x, "y": y, "z": z, "core": core}


def partners(level, member):
    pairs = []
    for at in places():
        to = dict(at)
        for i, (axis, pairing) in enumerate(GROUPS[at["core"]][level]):
            if member in ((1, 2), (1, 3))[i]:
                to[axis] = paired(to[axis], pairing)
        pairs.append((number(at), number(to)))
    return pairs


def other_core():
    return [(number(at), number({**at, "core": 1 - at["core"]})) for at in places()]


def rank_in(level, core, at):
    ranks = []
    for c in range(2):
        (a, pa), (b, pb) = GROUPS[c][level]
        u, v = pair_bit(at[a], pa), pair_bit(at[b], pb)
        ranks.append(2 * (u ^ v) + v)
    return jnp.where(core == 0, ranks[0], ranks[1])


def exchange(arrays, level, order=(1, 2, 3)):
    got = {m: lax.ppermute(arrays[m - 1], BOTH, partners(level, m)) for m in order}
    return [got[1], got[2], got[3]]


def after(value, *others):
    return lax.optimization_barrier((value, *others))[0]


def call(kernel, outs, *args, scratch=(), aliases=None, cost=FREE):
    return pl.pallas_call(
        kernel,
        out_shape=list(outs),
        in_specs=[SMEM if a.dtype == jnp.int32 and a.size < 100 else VMEM for a in args],
        out_specs=[VMEM] * len(outs),
        scratch_shapes=list(scratch),
        input_output_aliases=aliases or {},
        compiler_params=PARAMS,
        cost_estimate=cost,
    )(*args)


def shape(dims, dtype):
    return jax.ShapeDtypeStruct(dims, dtype)


def put_coded(read, ref, index):
    row = lax.broadcasted_iota(jnp.int32, (16, C), 0)
    exponents = jnp.zeros((16, C), jnp.float32)
    for b in range(BLOCKS):
        x = read(b)
        top = jnp.max(jnp.abs(x), axis=0, keepdims=True)
        e = jnp.ceil(jnp.log2(jnp.maximum(top, 2.0**-110)))
        q = jnp.clip(jnp.round(x * jnp.exp2(15.0 - e)), -32767.0, 32767.0)
        ref[index, b * BLOCK : (b + 1) * BLOCK, :] = q.astype(jnp.int16)
        exponents = jnp.where(row == b, e, exponents)
    ref[index, ROWS:CODED, :] = exponents.astype(jnp.int16)


def coded_scales(ref, index):
    return jnp.exp2(ref[index, ROWS:CODED, :].astype(jnp.float32) - 15.0)


def block_of(ref, index, b):
    return ref[index, b * BLOCK : (b + 1) * BLOCK, :]


def coded_block(ref, index, scales, b):
    return block_of(ref, index, b).astype(jnp.float32) * scales[b : b + 1, :]


def pair_sum_kernel(last, own, got, out):
    for c in range(4):
        scales = coded_scales(got, c)

        def read(b, c=c, scales=scales):
            rows = slice(c * ROWS + b * BLOCK, c * ROWS + (b + 1) * BLOCK)
            return own[rows, :] + coded_block(got, c, scales, b)

        if last:
            for b in range(BLOCKS):
                out[c, b * BLOCK : (b + 1) * BLOCK, :] = read(b)
        else:
            put_coded(read, out, c)


def group_sum_kernel(rank, own, got_1, got_2, got_3, keep, first, second, third):
    g = rank[0]
    for m, out in enumerate((keep, first, second, third)):
        at = g ^ m
        scales = [coded_scales(r, at) for r in (got_1, got_2, got_3)]

        def read(b, at=at, scales=scales):
            x = block_of(own, at, b)
            for r, s in zip((got_1, got_2, got_3), scales):
                x = x + coded_block(r, at, s, b)
            return x

        if m == 0:
            for b in range(BLOCKS):
                out[0, b * BLOCK : (b + 1) * BLOCK, :] = read(b)
        else:
            put_coded(read, out, 0)


def last_group_kernel(own, got_1, got_2, got_3, out):
    scales = [coded_scales(r, 0) for r in (got_1, got_2, got_3)]

    def read(b):
        x = block_of(own, 0, b)
        for r, s in zip((got_1, got_2, got_3), scales):
            x = x + coded_block(r, 0, s, b)
        return x

    put_coded(read, out, 0)


def total_kernel(own, got_1, got_2, got_3, out):
    refs = (own, got_1, got_2, got_3)
    scales = [coded_scales(r, 0) for r in refs]

    def read(b):
        a = [coded_block(r, 0, s, b) for r, s in zip(refs, scales)]
        return (a[0] + a[1]) + (a[2] + a[3])

    put_coded(read, out, 0)


def finish_kernel(scale, parts, where, *refs):
    n = len(parts)
    out, stage, done = refs[-3:]

    def copy_of(s, j):
        side, member = parts[s]
        k = (where[2 + side] ^ member) * EACH + j
        rows = pl.ds(pl.multiple_of((where[0] ^ side) * HALF, HALF), HALF)
        copy = pltpu.make_async_copy(stage.at[s, j], out.at[jnp.minimum(k, K - 1), rows, :], done.at[s, j])
        return k, copy

    def each(s, j, act):
        k, copy = copy_of(s, j)
        if j < EACH - 1:
            act(copy)
        else:
            pl.when(k < K)(lambda: act(copy))

    for s in range(n):
        for place in range(4):
            c = where[4 + parts[s][0]] ^ place
            scales = coded_scales(refs[s], c) * scale
            for b in range(BLOCKS):
                at = place * BLOCKS + b
                stage[s, at // 4, at % 4 * BLOCK : (at % 4 + 1) * BLOCK, :] = coded_block(refs[s], c, scales, b)
                if at % 4 == 3:
                    each(s, at // 4, lambda copy: copy.start())
    for s in range(n):
        for j in range(EACH):
            each(s, j, lambda copy: copy.wait())


def finish(scale, where, parts, sets, before):
    more = [] if before is None else [before]
    n = len(sets)
    return pl.pallas_call(
        functools.partial(finish_kernel, scale, parts),
        out_shape=shape((K, C, C), jnp.float32),
        in_specs=[SMEM] + [VMEM] * n + [HBM] * len(more),
        out_specs=HBM,
        scratch_shapes=[pltpu.VMEM((n, EACH, HALF, C), jnp.float32), pltpu.SemaphoreType.DMA((n, EACH))],
        input_output_aliases={1 + n: 0} if more else {},
        compiler_params=PARAMS,
        cost_estimate=FREE,
    )(where, *sets, *more)


def prepare_kernel(odd, features, cotangent, occupancy, cells, grad, masks, x_a, x_b, y_a, y_b):
    r = lax.broadcasted_iota(jnp.int32, (128, 128), 0)
    c = lax.broadcasted_iota(jnp.int32, (128, 128), 1)
    same = (r >> 4 == (c >> 3) & 7) & ((r >> 3) & 1 == c >> 6) & (r & 7 == c & 7)
    low = lax.broadcasted_iota(jnp.int32, (1, 128), 1) < 64
    occupied = occupancy[...].astype(jnp.float32)
    turned = pltpu.roll(occupied, 64, 1)
    even, core_0 = odd[0] == 0, odd[1] == 0
    ends = {}
    for x in range(8):
        lanes = slice(128 * (x // 2), 128 * (x // 2) + 128)
        if x % 2 == 0:
            row = jnp.where(low, occupied[0:1, lanes], turned[1:2, lanes])
        else:
            after_it = slice((lanes.start + 128) % 512, (lanes.start + 128) % 512 + 128)
            row = jnp.where(low, turned[0:1, after_it], occupied[1:2, lanes])
        pick = jnp.where(same, row, 0.0).astype(jnp.bfloat16)
        masks[x] = pick
        for index, (source, out) in enumerate(((features, cells), (cotangent, grad))):
            layer = jnp.concatenate([source[0, x], source[1, x]], axis=0)
            made = jnp.dot(pick, layer, preferred_element_type=jnp.float32).astype(jnp.bfloat16)
            made = made.reshape(8, 16, C)
            out[x] = made
            y_a[index, x] = jnp.where(even, made[7], made[0])
            y_b[index, x] = jnp.where(even, made[0], made[7])
            ends[index, x] = made
    for index in range(2):
        x_a[index] = jnp.where(core_0, ends[index, 7], ends[index, 0])
        x_b[index] = jnp.where(core_0, ends[index, 0], ends[index, 7])


def picks_kernel(neighbors, out):
    c = lax.broadcasted_iota(jnp.int32, (160, 160), 1)
    r = lax.broadcasted_iota(jnp.int32, (160, 1), 0)
    y, s, z = r >> 4, (r >> 3) & 1, r & 7
    side_y = jnp.where(y == 0, 0, jnp.where(y == 9, 2, 1))
    which = side_y * 2 + s
    for ox in range(3):
        for oz in range(3):
            edge = z == (0 if oz == 0 else 7)
            slot = jnp.full((160, 1), -1, jnp.int32)
            for oy in range(3):
                for brick in range(2):
                    level = neighbors[brick, 9 * ox + 3 * oy + 1]
                    beyond = neighbors[brick, 9 * ox + 3 * oy + oz]
                    found = jnp.where(edge, beyond, level) if oz != 1 else level
                    slot = jnp.where(which == 2 * oy + brick, found, slot)
            target = jnp.where(slot >= 0, y * 16 + slot * 8 + ((z + oz - 1) & 7), -1)
            out[ox, 160 * oz : 160 * (oz + 1), :] = jnp.where(c == target, 1.0, 0.0).astype(jnp.bfloat16)


def corners_kernel(odd, x_a, x_b, c_a, c_b):
    even = odd[0] == 0
    for side, x in enumerate((x_a, x_b)):
        for index in range(2):
            c_a[side, index] = jnp.where(even, x[index, 7], x[index, 0])
            c_b[side, index] = jnp.where(even, x[index, 0], x[index, 7])


def spread(pick, layer, x, wide):
    moved = jnp.dot(pick, layer, preferred_element_type=jnp.float32).astype(jnp.bfloat16)
    for oz in range(3):
        wide[oz, x] = moved[160 * oz : 160 * (oz + 1)].reshape(10, 16, C)


def widen_inner(index, odd, pick, cells, y_a, y_b, wide):
    even = odd[0] == 0
    for x in range(8):
        a, b = y_a[index, x], y_b[index, x]
        layer = [jnp.where(even, b, a), cells[x].reshape(128, C), jnp.where(even, a, b)]
        spread(pick[1], jnp.concatenate(layer, axis=0), x + 1, wide)


def widen_outer(index, odd, pick, x_a, x_b, c_a, c_b, wide):
    even, core_0 = odd[0] == 0, odd[1] == 0
    layers = []
    for side, x in enumerate((x_a, x_b)):
        a, b = c_a[side, index], c_b[side, index]
        rows = [jnp.where(even, b, a), x[index].reshape(128, C), jnp.where(even, a, b)]
        layers.append(jnp.concatenate(rows, axis=0))
    spread(pick[0], jnp.where(core_0, layers[1], layers[0]), 0, wide)
    spread(pick[2], jnp.where(core_0, layers[0], layers[1]), 9, wide)


def inner_kernel(odd, pick, cells, y_a, y_b, wide):
    widen_inner(0, odd, pick, cells, y_a, y_b, wide)


def outer_kernel(odd, pick, x_a, x_b, c_a, c_b, _, wide):
    widen_outer(0, odd, pick, x_a, x_b, c_a, c_b, wide)


def part_kernel(member, where, wide, grad, own, coded, terms):
    g = grad[...].reshape(1024, C)
    for j in range(EACH):
        sides = []
        for side in range(2):
            k = jnp.minimum((where[2 + side] ^ member) * EACH + j, K - 1)
            lanes = pl.ds(pl.multiple_of((where[0] ^ side) * HALF, HALF), HALF)
            w = wide[k % 3, pl.ds(k // 9, 8), pl.ds((k // 3) % 3, 8), :, lanes]
            sides.append(w.reshape(1024, HALF))
        t = lax.dot_general(
            jnp.concatenate(sides, axis=1), g, (((0,), (0,)), ((), ())), preferred_element_type=jnp.float32
        )
        own[j * HALF : (j + 1) * HALF, :] = t[:HALF]
        terms[j * HALF : (j + 1) * HALF, :] = t[HALF:]
    for c in range(4):
        put_coded(lambda b, c=c: terms[c * ROWS + b * BLOCK : c * ROWS + (b + 1) * BLOCK, :], coded, c)


def convolve(back, wide, kernel, masks, out, sums):
    for x in range(0, 8, 2):
        total = None
        for k in range(K):
            ox, oy, oz = k // 9, (k // 3) % 3, k % 3
            if back:
                ox, oy, oz = 2 - ox, 2 - oy, 2 - oz
            w = wide[oz, ox + x : ox + x + 2, oy : oy + 8].reshape(256, C)
            d = lax.dot_general(
                w, kernel[k], (((1,), (1 if back else 0,)), ((), ())), preferred_element_type=jnp.float32
            )
            total = d if total is None else total + d
        sums[x * 128 : (x + 2) * 128, :] = total.astype(jnp.bfloat16)
    for x in range(8):
        cells = lax.dot_general(
            masks[x], sums[x * 128 : (x + 1) * 128, :], (((0,), (0,)), ((), ())),
            preferred_element_type=jnp.float32,
        ).astype(jnp.bfloat16)
        out[0, x] = cells[:64]
        out[1, x] = cells[64:]


def forward_kernel(wide, kernel, masks, out, sums):
    convolve(False, wide, kernel, masks, out, sums)


def backward_kernel(odd, pick, grad, y_a, y_b, x_a, x_b, c_a, c_b, kernel, masks, out, sums, wide):
    widen_inner(1, odd, pick, grad, y_a, y_b, wide)
    widen_outer(1, odd, pick, x_a, x_b, c_a, c_b, wide)
    convolve(True, wide, kernel, masks, out, sums)


def shards(features, cotangent, kernel, occupancy, neighbors):
    gx, gy = lax.axis_index("gx"), lax.axis_index("gy")
    core = gx % 2
    at = {"x": gy, "y": gx // 8, "z": (gx // 2) % 4}
    scale = 1.0 / (512.0 * 256.0) ** 0.5
    outer, inner = rank_in(0, core, at), rank_in(1, core, at)
    where = jnp.stack([core, inner, outer, rank_in(0, 1 - core, at), inner, rank_in(1, 1 - core, at)])
    where = where.astype(jnp.int32)

    odd = jnp.stack([gy % 2, core]).astype(jnp.int32)

    y_pairs = ([(0, 1), (1, 0), (2, 3), (3, 2)], [(1, 2), (2, 1)])
    x_pairs = ([(i, i ^ 1) for i in range(32)], [(i, i + 1 if i % 2 else i - 1) for i in range(1, 31)])

    column = shape((8, 8, 16, C), jnp.bfloat16)
    wide_shape = (3, 10, 10, 16, C)
    side = shape((2, 8, 16, C), jnp.bfloat16)
    corner = shape((2, 2, 16, C), jnp.bfloat16)

    def swap(arrays, axis, pairs):
        return [lax.ppermute(a, axis, p) for a, p in zip(arrays, pairs)]

    busy = pl.CostEstimate(flops=2**31, bytes_accessed=2**22, transcendentals=0)
    (pick,) = call(picks_kernel, [shape((3, 480, 160), jnp.bfloat16)], neighbors, cost=busy)
    odd = after(odd, pick)
    cells, grad, masks, x_a, x_b, y_a, y_b = call(
        prepare_kernel,
        [column, column, shape((8, 128, 128), jnp.bfloat16)] + [side] * 4,
        odd, features.reshape(2, 8, 64, C), cotangent.reshape(2, 8, 64, C), occupancy,
    )
    x_halo = swap((x_a, x_b), "gx", x_pairs)
    y_halo = swap((after(y_a, x_halo[0]), after(y_b, x_halo[0])), "gy", y_pairs)
    corners = swap(call(corners_kernel, [corner, corner], odd, *x_halo), "gy", y_pairs)
    (wide,) = call(inner_kernel, [shape(wide_shape, jnp.bfloat16)], odd, pick, cells, *y_halo)
    halo = (*x_halo, *corners)
    (wide,) = call(outer_kernel, [shape(wide_shape, jnp.bfloat16)], odd, pick, *halo, wide, aliases={6: 0})

    sums, got, before = {}, {}, []

    def part(m, *before):
        return call(
            functools.partial(part_kernel, m),
            [shape((EACH * HALF, C), jnp.float32), CODED_4],
            where, after(wide, *before), grad,
            scratch=[pltpu.VMEM((EACH * HALF, C), jnp.float32)],
        )

    def chip_sum(m, own, got):
        out = CODED_4 if m else shape((4, ROWS, C), jnp.float32)
        return call(functools.partial(pair_sum_kernel, m == 0), [out], own, got)[0]

    for m in (0, 1, 2, 3):
        own, coded = part(m, *before)
        sums[m] = chip_sum(m, own, lax.ppermute(coded, BOTH, other_core()))
        before = [own] + list(sums.values())[-2:-1]
        if m:
            got[m] = lax.ppermute(sums[m], BOTH, partners(0, m))
    brick_rows = shape((2, 8, 64, C), jnp.bfloat16)
    totals = pltpu.VMEM((1024, C), jnp.bfloat16)
    (forward,) = call(forward_kernel, [brick_rows], after(wide, sums[3]), kernel, masks, scratch=[totals])
    keep, *sent = call(
        group_sum_kernel,
        [shape((1, ROWS, C), jnp.float32)] + [CODED_1] * 3,
        inner.reshape(1).astype(jnp.int32), after(sums[0], forward), got[1], got[2], got[3],
    )
    (partial,) = call(last_group_kernel, [CODED_1], keep, *exchange(sent, 1))
    (whole,) = call(total_kernel, [CODED_1], partial, *exchange([partial] * 3, 2, (2, 3, 1)))
    four = jnp.concatenate([whole] + exchange([whole] * 3, 1, (2, 3, 1)))
    sets = [four] + exchange([four] * 3, 0)

    (backward,) = call(
        backward_kernel, [brick_rows], odd, pick, after(grad, four), *y_halo, *halo, kernel, masks,
        scratch=[totals, pltpu.VMEM(wide_shape, jnp.bfloat16)],
    )

    def other(a):
        return lax.ppermute(a, BOTH, other_core())

    done = finish(scale, where, [(0, 0)], [after(four, backward)], None)
    *own, done = lax.optimization_barrier((*sets, done))
    far = [other(a) for a in own]
    done = finish(scale, where, [(0, 1), (0, 2), (0, 3)], own[1:], done)
    done = finish(scale, where, [(1, 0), (1, 1), (1, 2), (1, 3)], far, done)
    return forward.reshape(2, 8, 8, 8, C), backward.reshape(2, 8, 8, 8, C), done


def solution(mesh):
    placed = (
        P(BOTH, None, None, None, None),
        P(BOTH, None, None, None, None),
        P(),
        P(BOTH, None),
        P(BOTH, None),
    )
    return jax.shard_map(
        shards,
        mesh=mesh,
        in_specs=placed,
        out_specs=(P(BOTH, None, None, None, None), P(BOTH, None, None, None, None), P()),
        check_vma=False,
    )
```
